32 devices in a mesh: dp: 8 (over y, x, core), tensor: 4 (over z).
Axes of the slice: x: 2, y: 2, z: 4, core: 2. Of those that a mesh axis runs over, the one named last changes fastest.
Arguments:
- tokens: bfloat16 [16384, 768], P(('dp', 'tensor')), may hold values from -6 to 6
- cotangent: bfloat16 [16384, 768], P(('dp', 'tensor')), may hold values from -6 to 6
- routes: int32 [16384, 2], P('dp'), may hold values from 0 to 7, all different within a row; in each aligned block of 1024 rows (0 to 1023, 1024 to 2047, ...) at most 320 rows name the same one
- gain_attention: bfloat16 [768], P(('dp', 'tensor')), may hold values from 0.5 to 1.5
- gain_experts: bfloat16 [768], P(('dp', 'tensor')), may hold values from 0.5 to 1.5
- router_weight: bfloat16 [768, 8], P(('dp', 'tensor')), may hold values from -0.15625 to 0.15625
- qkv_weight: bfloat16 [768, 3, 768], P('dp', None, 'tensor'), may hold values from -0.21875 to 0.21875
- proj_weight: bfloat16 [768, 768], P('tensor', 'dp'), may hold values from -0.75 to 0.75
- expert_in: bfloat16 [8, 768, 3072], P(None, 'dp', 'tensor'), may hold values from -0.21875 to 0.21875
- expert_back: bfloat16 [8, 3072, 768], P(None, 'tensor', 'dp'), may hold values from -0.109375 to 0.109375
Outputs:
- layer_out: float32 [16384, 768], P(('dp', 'tensor'))
- input_grad: float32 [16384, 768], P(('dp', 'tensor'))
- gain_attention_grad: float32 [768], P(('dp', 'tensor'))
- gain_experts_grad: float32 [768], P(('dp', 'tensor'))
- router_grad: float32 [768, 8], P(('dp', 'tensor'))
- qkv_grad: float32 [768, 3, 768], P('dp', None, 'tensor')
- proj_grad: float32 [768, 768], P('tensor', 'dp')
- in_grad: float32 [8, 768, 3072], P(None, 'dp', 'tensor')
- back_grad: float32 [8, 3072, 768], P(None, 'tensor', 'dp')
The draws below stay inside these ranges and needn't reach their ends.
Inputs may be any that keep to these rules, and one draw needn't show every extreme that they name: `routes`: within each sequence of 1024 rows no expert is named by more than 320 rows, a bound that some block reaches; the two experts of a row differ.
All inputs are finite; a program needn't handle non-finite values.
Results may differ from the reference program's by a relative error of at most 0.019.
Values may be sent and summed in bfloat16 or wider, within the bound.
No kernel may reach another device: no remote copies, remote signals or barrier semaphores. Data moves between devices by JAX's collectives and lax.ppermute only.
A program may use at most 256 MiB of HBM per device.

```python
import math
import jax
import jax.numpy as jnp
import numpy as np
from jax import lax

D = 768
HEADS = 12
DH = 64
FF = 3072
EXPERTS = 8
SEQ_LEN = 1024
HD = 768
CAP = 320
TOKENS = 16384


def spiked(drawn, key, source, target, shards_of, factor):
    owner, partner = [(jnp.arange(drawn.shape[axis_at]) // (drawn.shape[axis_at] // shards_of)).reshape([-1 if axis == axis_at else 1 for axis in range(drawn.ndim)]) for axis_at in (source, target)]
    chosen = jax.random.permutation(key, shards_of)[partner]
    strong = (owner == chosen) | (owner == (partner + shards_of // 2) % shards_of)
    return jnp.where(strong, factor * drawn, drawn)


def shard_levels(rng, dims, pieces, smallest, largest):
    def one(position, shards_of):
        steps = jax.random.uniform(jax.random.fold_in(jax.random.fold_in(rng, 6), position), (shards_of,), jnp.float32, smallest / len(pieces), largest / len(pieces))
        return jnp.repeat(jnp.exp(steps), dims[position] // shards_of).reshape((-1,) + (1,) * (len(dims) - position - 1))

    loudness = one(*pieces[0])
    for cut in pieces[1:]:
        loudness = loudness * one(*cut)
    return loudness


def shared_out(key, own, number, rows, count, top, bound, lean):
    order = jax.random.permutation(key, count)
    heavy_load, usual = portions_of(count, rows * top, bound, lean, True), portions_of(count, rows * top, bound, lean, False)
    places = jnp.arange(count)

    def named(lengths, offset_by):
        used = int((lengths > 0).sum())
        fixed = max(1, used // 4)
        moved = fixed + (places - fixed + offset_by * (used - fixed)) % max(1, count - fixed)
        return jnp.zeros((count,), jnp.int32).at[order[jnp.where(places < fixed, places, moved)]].set(jnp.asarray(lengths, jnp.int32))

    lengths = jnp.where(number % 4 == 0, named(heavy_load, number // 4), named(usual, number - number // 4 - 1))
    mixed = jax.random.permutation(jax.random.fold_in(own, 3), count)
    donor, taker = mixed[0:count // 2 * 2:2], mixed[1:count // 2 * 2:2]
    room = jnp.minimum(lengths[donor] - 1, bound - lengths[taker]) // 2
    room = jnp.where((donor == order[0]) | (taker == order[0]) | (lengths[taker] == 0), 0, jnp.maximum(room, 0))
    moved = jax.random.randint(jax.random.fold_in(own, 4), (count // 2,), 0, 1 << 20) % (room + 1)
    lengths = lengths.at[donor].add(-moved).at[taker].add(moved)
    labels = jnp.searchsorted(jnp.cumsum(lengths), jnp.arange(rows * top), side="right").astype(jnp.int32)
    listing = labels.reshape(top, rows).T
    listing = listing[jax.random.permutation(jax.random.fold_in(own, 1), rows)]
    offset_by = jax.random.randint(jax.random.fold_in(own, 2), (rows, 1), 0, top)
    return jnp.take_along_axis(listing, (jnp.arange(top)[None, :] + offset_by) % top, axis=1)


def portions_of(number_of, total, bound, skew, full):
    portions = [(1 << 20) // math.isqrt(rank ** skew) + 1 for rank in range(1, number_of + 1)]
    largest = bound if full else min(bound, max(-(-total // number_of), total * portions[0] // sum(portions)))
    least = 1 if total - largest >= number_of - 1 else 0
    given, surplus = [largest] + [least] * (number_of - 1), total - largest - least * (number_of - 1)
    while surplus > 0:
        candidates = [i for i in range(1, number_of) if given[i] < largest] or [i for i in range(1, number_of) if given[i] < bound]
        pool, left = sum([portions[i] for i in candidates]), surplus
        for i in candidates:
            extra = min(bound - given[i], max(1, left * portions[i] // pool), surplus)
            given[i] = given[i] + extra
            surplus = surplus - extra
    return np.array(given)


def normal_values(rng, shape, deviation, limit, pieces=(), kind=jnp.bfloat16):
    values = jax.random.normal(rng, shape, jnp.float32) * deviation
    if len(pieces) > 0:
        values = shard_levels(rng, shape, pieces, -0.22, 0.18) * values
    return jnp.clip(values, min=-limit, max=limit).astype(kind)


def noise_with(key, extent, spread, limit, pieces, heavy, kind=jnp.bfloat16):
    values = spread * jax.random.normal(key, extent, jnp.float32)
    if pieces:
        values = values * shard_levels(key, extent, pieces, -0.22, 0.18)
    return jnp.clip(spiked(values, jax.random.fold_in(key, 3), *heavy), -limit, limit).astype(kind)


def setup_inputs(seed: int = 0) -> dict:
    key_list = jax.random.split(jax.random.key(seed), 11)
    tokens = normal_values(key_list[0], (TOKENS, D), 1.0, 6.0, ((0, 32),))
    cotangent = noise_with(key_list[1], (TOKENS, D), 1.0, 6.0, ((0, 32),), (0, 1, 32, 2.75))
    routes_keys = jax.random.split(jax.random.fold_in(key_list[2], 1), TOKENS // SEQ_LEN)
    routes_turns = jax.random.permutation(jax.random.fold_in(key_list[2], 3), TOKENS // SEQ_LEN)
    routes = jax.vmap(lambda own, number: shared_out(jax.random.fold_in(key_list[2], 2), own, number, SEQ_LEN, EXPERTS, 2, CAP, 1))(routes_keys, routes_turns).reshape((TOKENS, 2))
    gain_attention = jnp.clip(1.0 + 0.1 * jax.random.normal(key_list[3], (D,), jnp.float32), 0.5, 1.5).astype(jnp.bfloat16)
    gain_experts = jnp.clip(1.0 + 0.1 * jax.random.normal(key_list[4], (D,), jnp.float32), 0.5, 1.5).astype(jnp.bfloat16)
    router_weight = normal_values(key_list[5], (D, EXPERTS), (2 * D) ** -0.5, 0.15625, ((0, 32),))
    qkv_weight = normal_values(key_list[6], (D, 3, HD), D ** -0.5, 0.21875, ((0, 8), (2, 4)))
    proj_weight = normal_values(key_list[7], (HD, D), DH ** -0.5, 0.75, ((0, 4), (1, 8)))
    expert_in = normal_values(key_list[8], (EXPERTS, D, FF), D ** -0.5, 0.21875, ((1, 8), (2, 4)))
    expert_back = normal_values(key_list[9], (EXPERTS, FF, D), FF ** -0.5, 0.109375, ((1, 4), (2, 8)))
    return dict(tokens=tokens, cotangent=cotangent, routes=routes, gain_attention=gain_attention, gain_experts=gain_experts, router_weight=router_weight, qkv_weight=qkv_weight, proj_weight=proj_weight, expert_in=expert_in, expert_back=expert_back)


epsilon = 1e-06
masked_score = -1e+30
highest = lax.Precision.HIGHEST

@jax.custom_vjp
def low(v):
    return lax.optimization_barrier(v.astype(jnp.bfloat16)).astype(jnp.float32)

@jax.custom_vjp
def low_back(v):
    return v

def low_keep(v):
    return (low(v), None)

def low_pass(kept, grad):
    return (grad,)

def back_keep(v):
    return (v, None)

def back_low(kept, grad):
    return (low(grad),)
low.defvjp(low_keep, low_pass)
low_back.defvjp(back_keep, back_low)

def norm_rows(series, scales):
    return series * lax.rsqrt(lax.optimization_barrier(jnp.mean(series * series, axis=-1, keepdims=True)) + epsilon) * scales

def slot_index(chosen):
    flat = chosen.reshape(-1)
    onehot = (flat[:, None] == jnp.arange(EXPERTS, dtype=jnp.int32)[None, :]).astype(jnp.int32)
    earlier = jnp.cumsum(onehot, axis=0) - onehot
    place = lax.optimization_barrier(jnp.sum(earlier * onehot, axis=1))
    return (flat * CAP + place).astype(jnp.int32)

def attention(query, keys, values):
    block_rows = min(512, SEQ_LEN)

    def one_block(item):
        piece, first_row = item
        scores = jnp.einsum('bhd,khd->hbk', piece, keys, precision=highest) * DH ** (-0.5)
        scores = low_back(scores)
        rows_here = first_row + jnp.arange(block_rows, dtype=jnp.int32)
        columns = jnp.arange(SEQ_LEN, dtype=jnp.int32)
        scores = jnp.where(columns[None, None, :] <= rows_here[None, :, None], scores, masked_score)
        weights = jax.nn.softmax(scores, axis=-1)
        return jnp.einsum('hbk,khd->bhd', low(weights), values, precision=highest)
    blocks = query.reshape(SEQ_LEN // block_rows, block_rows, HEADS, DH)
    firsts = jnp.arange(SEQ_LEN // block_rows, dtype=jnp.int32) * block_rows
    result = lax.map(jax.checkpoint(one_block), (blocks, firsts))
    return result.reshape(SEQ_LEN, HEADS * DH)

def layer(inputs, chosen, gain_attention, gain_experts, router_weight, qkv_weight, proj_weight, expert_in, expert_back):
    normed_in = low(norm_rows(inputs, gain_attention))
    projected = jnp.einsum('td,dcf->ctf', normed_in, qkv_weight, precision=highest)
    projected = low(low_back(projected))
    query = projected[0].reshape(SEQ_LEN, HEADS, DH)
    keys = projected[1].reshape(SEQ_LEN, HEADS, DH)
    values = projected[2].reshape(SEQ_LEN, HEADS, DH)
    context = low(low_back(attention(query, keys, values)))
    attn_out = low_back(jnp.dot(context, proj_weight, precision=highest))
    middle = inputs + attn_out
    moe_in = low(norm_rows(middle, gain_experts))
    logits = low_back(jnp.dot(moe_in, router_weight, precision=highest))
    gates = jax.nn.softmax(jnp.take_along_axis(logits, chosen, axis=1), axis=1)
    slots = slot_index(chosen)
    entries = 2 * SEQ_LEN
    entry_index = jnp.full((EXPERTS * CAP,), entries, jnp.int32).at[slots].set(jnp.arange(entries, dtype=jnp.int32))
    padded = jnp.concatenate([moe_in, jnp.zeros((1, D), jnp.float32)], axis=0)
    expert_rows = padded[entry_index // 2].reshape(EXPERTS, CAP, D)
    hidden = low_back(jnp.einsum('ecd,edf->ecf', expert_rows, expert_in, precision=highest))
    activated = low(jax.nn.gelu(hidden))
    expert_out = jnp.einsum('ecf,efd->ecd', activated, expert_back, precision=highest).reshape(EXPERTS * CAP, D)
    picked = low_back(expert_out[slots].reshape(SEQ_LEN, 2, D))
    return middle + lax.optimization_barrier(jnp.sum(gates[:, :, None] * picked, axis=1))

def reference(tokens, cotangent, routes, gain_attention, gain_experts, router_weight, qkv_weight, proj_weight, expert_in, expert_back):
    params = tuple((item.astype(jnp.float32) for item in (gain_attention, gain_experts, router_weight, qkv_weight, proj_weight, expert_in, expert_back)))
    inputs = tokens.astype(jnp.float32).reshape(-1, SEQ_LEN, D)
    upstream = cotangent.astype(jnp.float32).reshape(-1, SEQ_LEN, D)
    chosen_all = routes.reshape(-1, SEQ_LEN, 2)

    def one_sequence(totals, item):
        series, grads_in, chosen = item

        def closed(values, *weights):
            return layer(values, chosen, *weights)
        result, backward = jax.vjp(closed, series, *params)
        grads = backward(grads_in)
        totals = tuple((total + grad for total, grad in zip(totals, grads[1:])))
        return (totals, (result, grads[0]))
    zeros = tuple((jnp.zeros(item.shape, jnp.float32) for item in params))
    totals, (outputs, input_grads) = lax.scan(one_sequence, zeros, (inputs, upstream, chosen_all))
    return (outputs.reshape(-1, D), input_grads.reshape(-1, D), totals[0], totals[1], totals[2], totals[3], totals[4], totals[5], totals[6])
```

```python
import functools

import jax
import jax.numpy as jnp
from jax import lax
from jax.experimental import pallas as pl
from jax.experimental.pallas import tpu as pltpu
from jax.sharding import PartitionSpec as P

DH = 64
EXPERTS = 8
SEQ_LEN = 1024
CAP = 320
BLOCK = 256
LANES = 128

epsilon = 1e-06
masked_score = -1e30
vmem_bytes = 56 * 1024 * 1024

f32 = jnp.float32
bf16 = jnp.bfloat16
NT = (((1,), (1,)), ((), ()))
TN = (((0,), (0,)), ((), ()))


def norm_rows(series, scales):
    return series * lax.rsqrt(jnp.mean(series * series, axis=-1, keepdims=True) + epsilon) * scales


def norm_back(series, scales, upstream):
    factor = lax.rsqrt(jnp.mean(series * series, axis=-1, keepdims=True) + epsilon)
    normed = series * factor
    scaled = upstream * scales
    series_grad = factor * (scaled - normed * jnp.mean(scaled * normed, axis=-1, keepdims=True))
    return (series_grad, jnp.sum(upstream * normed, axis=0))


def dot(a, b, dims=None):
    if dims is None:
        dims = (((1,), (0,)), ((), ()))
    return lax.dot_general(a, b, dims, preferred_element_type=f32)


def head_masks(scale):
    lane = lax.broadcasted_iota(jnp.int32, (1, LANES), 1)
    return [
        jnp.where((lane >= head * DH) & (lane < (head + 1) * DH), scale, 0.0).astype(bf16)
        for head in range(LANES // DH)
    ]


def causal_block():
    shape = (BLOCK, BLOCK)
    return lax.broadcasted_iota(jnp.int32, shape, 0) <= lax.broadcasted_iota(jnp.int32, shape, 1)


def attend_forward_kernel(query, keys, values, context, log_totals):
    masks = head_masks(DH**-0.5)
    seen = causal_block()
    values_t = values[...].astype(f32).T.astype(bf16)
    for i in range(SEQ_LEN // BLOCK):
        rows = slice(i * BLOCK, (i + 1) * BLOCK)
        parts = []
        for head, mask in enumerate(masks):
            piece = query[rows, :] * mask
            scores = [
                dot(keys[j * BLOCK : (j + 1) * BLOCK, :], piece, NT) for j in range(i + 1)
            ]
            scores[i] = jnp.where(seen, scores[i], masked_score)
            largest = jnp.max(scores[0], axis=0, keepdims=True)
            for block in scores[1:]:
                largest = jnp.maximum(largest, jnp.max(block, axis=0, keepdims=True))
            raised = [jnp.exp(block - largest) for block in scores]
            total = jnp.sum(raised[0], axis=0, keepdims=True)
            for block in raised[1:]:
                total = total + jnp.sum(block, axis=0, keepdims=True)
            summed = dot(
                values_t[head * DH : (head + 1) * DH, : (i + 1) * BLOCK],
                jnp.concatenate([block.astype(bf16) for block in raised], axis=0),
            )
            parts.append(summed / total)
            log_totals[0, head : head + 1, rows] = largest + jnp.log(total)
        context[rows, :] = jnp.concatenate(parts, axis=0).T.astype(bf16)


def attend_forward(project):
    pairs = project.shape[1] // (3 * LANES)
    column = lambda c: pl.BlockSpec((SEQ_LEN, LANES), lambda g, c=c: (0, c * pairs + g))
    heads = LANES // DH
    return pl.pallas_call(
        attend_forward_kernel,
        grid=(pairs,),
        in_specs=[column(0), column(1), column(2)],
        out_specs=[
            pl.BlockSpec((SEQ_LEN, LANES), lambda g: (0, g)),
            pl.BlockSpec((1, heads, SEQ_LEN), lambda g: (g, 0, 0)),
        ],
        out_shape=[
            jax.ShapeDtypeStruct((SEQ_LEN, pairs * LANES), bf16),
            jax.ShapeDtypeStruct((pairs, heads, SEQ_LEN), f32),
        ],
        compiler_params=pltpu.CompilerParams(vmem_limit_bytes=vmem_bytes),
        cost_estimate=estimate(14 << 30, 4 << 20),
        name="attend_forward",
    )(project, project, project)


def attend_backward_kernel(pairs, query, keys, values, upstream, log_totals, grads, key_sum, value_sum):
    g = pl.program_id(0)
    scaled_masks = head_masks(DH**-0.5)
    masks = head_masks(1.0)
    seen = causal_block()
    keys_t = keys[...].astype(f32).T.astype(bf16)
    key_sum[...] = jnp.zeros_like(key_sum)
    value_sum[...] = jnp.zeros_like(value_sum)
    for i in range(SEQ_LEN // BLOCK):
        rows = slice(i * BLOCK, (i + 1) * BLOCK)
        parts = []
        for head in range(LANES // DH):
            piece = query[rows, :] * scaled_masks[head]
            above = upstream[rows, :] * masks[head]
            log_total = log_totals[0, head : head + 1, rows]
            weights, probs = [], []
            inner = jnp.zeros((1, BLOCK), f32)
            for j in range(i + 1):
                columns = slice(j * BLOCK, (j + 1) * BLOCK)
                scores = dot(keys[columns, :], piece, NT)
                if j == i:
                    scores = jnp.where(seen, scores, masked_score)
                weights.append(jnp.exp(scores - log_total))
                probs.append(dot(values[columns, :], above, NT))
                inner = inner + jnp.sum(weights[j] * probs[j], axis=0, keepdims=True)
            score_grads = []
            for j in range(i + 1):
                score_grads.append((weights[j] * (probs[j] - inner)).astype(bf16))
            length = (i + 1) * BLOCK
            all_grads = jnp.concatenate(score_grads, axis=0)
            all_weights = jnp.concatenate([block.astype(bf16) for block in weights], axis=0)
            value_sum[:length, :] += dot(all_weights, above)
            key_sum[:length, :] += dot(all_grads, piece)
            parts.append(dot(keys_t[head * DH : (head + 1) * DH, :length], all_grads))
        query_grad = jnp.concatenate(parts, axis=0).T * DH**-0.5
        grads[rows, pl.ds(pl.multiple_of(g * LANES, LANES), LANES)] = query_grad.astype(bf16)
    grads[:, pl.ds(pl.multiple_of((pairs + g) * LANES, LANES), LANES)] = key_sum[...].astype(bf16)
    grads[:, pl.ds(pl.multiple_of((2 * pairs + g) * LANES, LANES), LANES)] = value_sum[...].astype(
        bf16
    )


def attend_backward(project, upstream, log_totals):
    pairs = project.shape[1] // (3 * LANES)
    column = lambda c: pl.BlockSpec((SEQ_LEN, LANES), lambda g, c=c: (0, c * pairs + g))
    heads = LANES // DH
    return pl.pallas_call(
        functools.partial(attend_backward_kernel, pairs),
        grid=(pairs,),
        in_specs=[
            column(0),
            column(1),
            column(2),
            column(0),
            pl.BlockSpec((1, heads, SEQ_LEN), lambda g: (g, 0, 0)),
        ],
        out_specs=pl.BlockSpec(project.shape, lambda g: (0, 0)),
        out_shape=jax.ShapeDtypeStruct(project.shape, bf16),
        scratch_shapes=[pltpu.VMEM((SEQ_LEN, LANES), f32), pltpu.VMEM((SEQ_LEN, LANES), f32)],
        compiler_params=pltpu.CompilerParams(vmem_limit_bytes=vmem_bytes),
        cost_estimate=estimate(20 << 30, 8 << 20),
        name="attend_backward",
    )(project, project, project, upstream, log_totals)


def slot_hits(place):
    return lax.broadcasted_iota(jnp.int32, (CAP, SEQ_LEN), 0) == place.astype(jnp.int32)


GROUP = 4


def keep_term(expert, onehots, terms, onehot, term):
    rows = pl.ds(pl.multiple_of(expert % GROUP * CAP, 64), CAP)
    onehots[rows, :] = onehot
    terms[rows, :] = term


def add_terms(expert, onehots, terms, total, results):
    @pl.when(expert % GROUP == GROUP - 1)
    def _():
        for i in range(SEQ_LEN // BLOCK):
            rows = slice(i * BLOCK, (i + 1) * BLOCK)
            term = dot(onehots[:, rows], terms[...], TN)

            @pl.when(expert == GROUP - 1)
            def _():
                total[rows, :] = term

            @pl.when(expert == EXPERTS - 1)
            def _():
                result = results[i // (SEQ_LEN // BLOCK // 2)]
                first = i % (SEQ_LEN // BLOCK // 2) * BLOCK
                result[first : first + BLOCK, :] = (total[rows, :] + term).astype(bf16)


def combine_scratch(width):
    return [
        pltpu.VMEM((GROUP * CAP, SEQ_LEN), bf16),
        pltpu.VMEM((GROUP * CAP, width), bf16),
        pltpu.VMEM((SEQ_LEN, width), f32),
    ]


def assemble(me, offsets, blocks, weight):
    rows = weight.shape[0] // len(offsets)
    for i, offset in enumerate(offsets):
        start = 0 if len(offsets) == 1 else pl.multiple_of((me ^ offset) * rows, 16)
        weight[pl.ds(start, rows), :] = blocks[i][0]


def fill(edge, parts, whole):
    rows = SEQ_LEN // 2
    for i, choices in enumerate(parts):
        target = slice(i * rows, (i + 1) * rows)
        if len(choices) == 1:
            whole[target, :] = choices[0][...]
            continue

        @pl.when(edge == 1)
        def _():
            whole[target, :] = choices[0][...]

        @pl.when(edge == 0)
        def _():
            whole[target, :] = choices[1][...]


def expert_kernel(offsets, choices, place_info, place, router, *refs):
    count = len(offsets[0])
    groups = []
    for _ in range(4):
        groups.append(refs[:choices])
        refs = refs[choices:]
    first_blocks, second_blocks = refs[:count], refs[count : 2 * count]
    back, back_two, gates, slots_in, slots_grad, activated, hidden_grad = refs[
        2 * count : 2 * count + 7
    ]
    onehots, terms, total, first, second, gate_grad, rows, upstream = refs[2 * count + 7 :]
    expert = pl.program_id(0)
    assemble(place_info[0], offsets[0], first_blocks, first)
    assemble(place_info[0], offsets[1], second_blocks, second)

    @pl.when(expert == 0)
    def _():
        fill(place_info[1], groups[:2], rows)
        fill(place_info[1], groups[2:], upstream)
        logits = dot(router[...], rows[...], NT)
        chosen = place[...] >= 0.0
        largest = jnp.max(jnp.where(chosen, logits, masked_score), axis=0, keepdims=True)
        raised = jnp.where(chosen, jnp.exp(jnp.where(chosen, logits - largest, 0.0)), 0.0)
        gates[...] = raised / jnp.sum(raised, axis=0, keepdims=True)

    row = pl.ds(expert, 1)
    hits = slot_hits(place[row, :])
    onehot = jnp.where(hits, 1.0, 0.0).astype(bf16)
    entered = dot(onehot, rows[...]).astype(bf16)
    above = dot(onehot, upstream[...]).astype(bf16)
    slot_gate = jnp.sum(jnp.where(hits, gates[row, :], 0.0), axis=1, keepdims=True)
    hidden = dot(entered, first[...])
    raw_grad = dot(above, second[...])
    slots_in[0] = entered
    slots_grad[0] = above
    square = hidden * hidden
    factor = 0.7978845608028654
    bent = jnp.tanh(factor * hidden * (1.0 + 0.044715 * square))
    half = 0.5 * (1.0 + bent)
    active = (hidden * half).astype(bf16)
    slope = half + 0.5 * hidden * (1.0 - bent * bent) * (factor * (1.0 + 3 * 0.044715 * square))
    activated[0] = (slot_gate * active.astype(f32)).astype(bf16)
    slot_gate_grad = jnp.sum(active.astype(f32) * raw_grad, axis=1, keepdims=True)
    gate_grad[row, :] = jnp.sum(jnp.where(hits, slot_gate_grad, 0.0), axis=0, keepdims=True)
    below = (slot_gate * raw_grad * slope).astype(bf16)
    hidden_grad[0] = below
    slot_back = dot(below, first[...], NT).astype(bf16)
    keep_term(expert, onehots, terms, onehot, slot_back)
    add_terms(expert, onehots, terms, total, (back, back_two))

    @pl.when(expert == EXPERTS - 1)
    def _():
        half = SEQ_LEN // 2
        for i, result in enumerate((back, back_two)):
            result[half:, :] = jnp.zeros((result.shape[0] - half, result.shape[1]), bf16)
            grads = gate_grad[:, i * half : (i + 1) * half]
            result[half:, :half] = jnp.concatenate([grads, jnp.zeros_like(grads)], 0).astype(bf16)


def block_specs(blocks):
    return [pl.BlockSpec((1,) + block.shape[1:], lambda e: (e, 0, 0)) for block in blocks]


def estimate(flops, moved):
    return pl.CostEstimate(flops=flops, bytes_accessed=moved, transcendentals=0)


scalar = pl.BlockSpec(memory_space=pltpu.SMEM)


def through_experts(place_info, place, router, row_parts, upstream_parts, first, second):
    parts = row_parts + upstream_parts
    choices = len(parts[0])
    half, width = parts[0][0].shape
    hidden_width = first[1][0].shape[2]
    line = pl.BlockSpec((EXPERTS, SEQ_LEN), lambda e: (0, 0))
    whole = pl.BlockSpec((half, width), lambda e: (0, 0))
    under = pl.BlockSpec((half + 16, width), lambda e: (0, 0))
    slots = lambda columns: pl.BlockSpec((1, CAP, columns), lambda e: (e, 0, 0))
    slot_shape = lambda columns: jax.ShapeDtypeStruct((EXPERTS, CAP, columns), bf16)
    return pl.pallas_call(
        functools.partial(expert_kernel, (first[0], second[0]), choices),
        grid=(EXPERTS,),
        in_specs=[scalar, line, pl.BlockSpec((EXPERTS, width), lambda e: (0, 0))]
        + [whole] * (4 * choices)
        + block_specs(first[1])
        + block_specs(second[1]),
        out_specs=[
            under,
            under,
            line,
            slots(width),
            slots(width),
            slots(hidden_width),
            slots(hidden_width),
        ],
        out_shape=[
            jax.ShapeDtypeStruct((half + 16, width), bf16),
            jax.ShapeDtypeStruct((half + 16, width), bf16),
            jax.ShapeDtypeStruct((EXPERTS, SEQ_LEN), f32),
            slot_shape(width),
            slot_shape(width),
            slot_shape(hidden_width),
            slot_shape(hidden_width),
        ],
        scratch_shapes=combine_scratch(width)
        + [
            pltpu.VMEM((width, hidden_width), bf16),
            pltpu.VMEM((width, hidden_width), bf16),
            pltpu.VMEM((EXPERTS, SEQ_LEN), f32),
            pltpu.VMEM((SEQ_LEN, width), bf16),
            pltpu.VMEM((SEQ_LEN, width), bf16),
        ],
        compiler_params=pltpu.CompilerParams(vmem_limit_bytes=vmem_bytes),
        cost_estimate=estimate(60 << 30, 50 << 20),
        name="through_experts",
    )(place_info, place, router, *[item for part in parts for item in part], *first[1], *second[1])


def grads_kernel(count, parts, place_info, *refs):
    slots_in, slots_grad, activated, hidden_grad = [
        jnp.concatenate([ref[0] for ref in refs[i * count : (i + 1) * count]], axis=0)
        for i in range(4)
    ]
    outs = refs[4 * count :]
    even = (place_info[0] & 1) == 0
    for i, (left, right) in enumerate(((slots_in, hidden_grad), (slots_grad, activated))):
        product = dot(left, right, TN)
        if parts == 1:
            outs[i][0, 0] = product.astype(bf16)
            continue
        rows = product.shape[0] // parts
        for j in range(parts // 2):
            one = product[2 * j * rows : (2 * j + 1) * rows]
            two = product[(2 * j + 1) * rows : (2 * j + 2) * rows]
            outs[2 * i][0, j] = jnp.where(even, one, two).astype(bf16)
            outs[2 * i + 1][0, j] = jnp.where(even, two, one).astype(bf16)


def expert_grads(place_info, sequences, parts):
    count = len(sequences)
    width, hidden_width = sequences[0][0].shape[2], sequences[0][2].shape[2]
    slots = lambda columns: pl.BlockSpec((1, CAP, columns), lambda e: (e, 0, 0))
    specs = [slots(width), slots(width), slots(hidden_width), slots(hidden_width)]
    shape = (max(parts // 2, 1), width // parts, hidden_width)
    outs = 2 * min(parts, 2)
    return pl.pallas_call(
        functools.partial(grads_kernel, count, parts),
        grid=(EXPERTS,),
        in_specs=[scalar] + [spec for spec in specs for _ in range(count)],
        out_specs=[pl.BlockSpec((1,) + shape, lambda e: (e, 0, 0, 0))] * outs,
        out_shape=[jax.ShapeDtypeStruct((EXPERTS,) + shape, bf16)] * outs,
        compiler_params=pltpu.CompilerParams(vmem_limit_bytes=vmem_bytes),
        cost_estimate=estimate(50 << 30, 50 << 20),
        name="expert_grads",
    )(place_info, *[item[i] for i in range(4) for item in sequences])


def outputs_kernel(count, offsets, place_info, *refs):
    expert = pl.program_id(0)
    blocks_count = len(offsets)
    place, activated = refs[:count], refs[count : 2 * count]
    blocks = refs[2 * count : 2 * count + blocks_count]
    refs = refs[2 * count + blocks_count :]
    second = refs[-1]
    assemble(place_info[0], offsets, blocks, second)
    for s in range(count):
        hits = slot_hits(place[s][pl.ds(expert, 1), :])
        out = dot(activated[s][0], second[...], NT).astype(bf16)
        onehot = jnp.where(hits, 1.0, 0.0).astype(bf16)
        onehots, terms, total = refs[2 * count + 3 * s : 2 * count + 3 * s + 3]
        keep_term(expert, onehots, terms, onehot, out)
        add_terms(expert, onehots, terms, total, refs[2 * s : 2 * s + 2])


def expert_outputs(place_info, places, activated, second):
    count = len(places)
    hidden_width = second[1][0].shape[2]
    width = second[1][0].shape[1] * len(second[0])
    half = SEQ_LEN // 2
    line = pl.BlockSpec((EXPERTS, SEQ_LEN), lambda e: (0, 0))
    whole = pl.BlockSpec((half, width), lambda e: (0, 0))
    slots = pl.BlockSpec((1, CAP, hidden_width), lambda e: (e, 0, 0))
    return pl.pallas_call(
        functools.partial(outputs_kernel, count, second[0]),
        grid=(EXPERTS,),
        in_specs=[scalar] + [line] * count + [slots] * count + block_specs(second[1]),
        out_specs=[whole] * (2 * count),
        out_shape=[jax.ShapeDtypeStruct((half, width), bf16)] * (2 * count),
        scratch_shapes=combine_scratch(width) * count + [pltpu.VMEM((width, hidden_width), bf16)],
        compiler_params=pltpu.CompilerParams(vmem_limit_bytes=vmem_bytes),
        cost_estimate=estimate(60 << 30, 30 << 20),
        name="expert_outputs",
    )(place_info, *places, *activated, *second[1])


def from_partner(value, distance):
    return lax.ppermute(value, "tensor", [(i, i ^ distance) for i in range(4)])


def between(value, *pairs):
    return lax.ppermute(value, "tensor", list(pairs))


def from_group(value, distance):
    count = lax.axis_size("dp")
    return lax.ppermute(value, "dp", [(i, i ^ distance) for i in range(count)])


def after(value, *others):
    return lax.optimization_barrier((value,) + others)[0]


def all_after(values, *others):
    return lax.optimization_barrier(tuple(values) + others)[: len(values)]


def summed(items):
    total = items[0].astype(f32)
    for item in items[1:]:
        total = total + item.astype(f32)
    return total


def spread_near(mine):
    return (mine, from_partner(mine, 1), between(mine, (1, 2), (2, 1)))


def spread_far(near):
    mine, partner, middle = near
    far = between(after(mine, partner, middle), (0, 3), (3, 0))
    return (
        between(middle, (1, 0), (2, 3)),
        between(partner, (1, 2), (2, 1)),
        far,
        middle,
    )


def collect_start(two, three):
    far = between(three, (0, 3), (3, 0))
    inward = between(two, (0, 1), (3, 2))
    across = between(two, (1, 2), (2, 1))
    return far, inward, across


def collect_middle(three, started):
    return between(summed([three, started[1]]).astype(bf16), (1, 2), (2, 1))


def collect_end(mine, partner, started, middle, edge):
    far, _, across = started
    partner = jnp.where(edge, partner, summed([partner, across]).astype(bf16))
    received = from_partner(partner, 1)
    return summed([mine, received, jnp.where(edge, far, middle)])


def grouped(block):
    return lax.axis_size("dp") == 8 and block.shape[1] % 16 == 0


def gathered(blocks):
    if len(blocks) > 1:
        blocks.update({offset ^ 1: from_group(item, 1) for offset, item in list(blocks.items())})
    return (tuple(blocks), list(blocks.values()))


def scatter_step(me, items, axis, distance):
    bit = (me // distance) & 1
    take = lambda item, which: lax.dynamic_index_in_dim(item, which, axis, keepdims=False)
    sent = summed([take(item, 1 - bit) for item in items]).astype(bf16)
    return [take(item, bit) for item in items], sent


def scatter_start(me, kept, received, way):
    items = [item.reshape((EXPERTS, 2, 2) + item.shape[2:]) for item in (kept, received)]
    return scatter_step(me, items, 1 if way[0] == 4 else 2, way[0])


def shards(
    tokens,
    cotangent,
    routes,
    gain_attention,
    gain_experts,
    router_weight,
    qkv_weight,
    proj_weight,
    expert_in,
    expert_back,
):
    local_rows, width = tokens.shape
    group_rows = routes.shape[0]
    sequences = group_rows // SEQ_LEN
    depth, _, quarter = qkv_weight.shape
    part = depth // 4
    side = 2 * quarter
    place_z = lax.axis_index("tensor")
    me = lax.axis_index("dp")
    odd = (place_z & 1) == 1
    low = place_z < 2
    half = place_z & 1
    edge = (place_z == 0) | (place_z == 3)

    def ordered(mine, other):
        return jnp.where(
            odd,
            jnp.concatenate([other, mine], axis=0),
            jnp.concatenate([mine, other], axis=0),
        )

    small = jnp.concatenate([gain_attention[:, None], gain_experts[:, None], router_weight], axis=1)
    small = jnp.pad(small, ((0, depth - part), (0, LANES - small.shape[1])))
    mine = qkv_weight.reshape(depth, 3 * quarter)
    small = small[:part]
    across = from_partner(mine, 2)
    smalls = [small] + [from_partner(small, distance) for distance in (1, 2, 3)]
    pick = lambda items: (
        jnp.where(low, items[0], items[2]),
        jnp.where(low, items[2], items[0]),
        jnp.where(low, items[1], items[3]),
        jnp.where(low, items[3], items[1]),
    )
    smalls = pick(smalls)
    smalls = jnp.where(
        odd,
        jnp.concatenate([smalls[2], smalls[0], smalls[3], smalls[1]], axis=0),
        jnp.concatenate([smalls[0], smalls[2], smalls[1], smalls[3]], axis=0),
    )
    one = jnp.where(low, mine, across).reshape(depth, 3, quarter)
    two = jnp.where(low, across, mine).reshape(depth, 3, quarter)
    packed = jnp.concatenate(
        [jnp.concatenate([one, two], axis=2).reshape(depth, 3 * side), smalls], axis=1
    )
    ways = ((2, 4), (4, 2))
    blocks = [expert_in, expert_back.transpose(0, 2, 1)]
    split = grouped(blocks[0])
    if split:
        crossed = [from_group(block, way[0]) for block, way in zip(blocks, ways)]
    packed = lax.all_gather(packed, "dp", axis=0, tiled=True)
    qkv_matrix = packed[:, : 3 * side]
    small = packed[:, 3 * side :]
    attn_gain = small[:, 0].astype(f32)
    moe_gain = small[:, 1].astype(f32)
    router = small[:, 2 : 2 + EXPERTS]
    token_partner = from_partner(after(tokens, across), 1)
    projection = after(proj_weight.T, token_partner)
    projections = [projection] + [from_partner(projection, distance) for distance in (1, 2, 3)]
    proj_matrix = jnp.concatenate(pick(projections), axis=1)
    proj_matrix = lax.all_gather(proj_matrix, "dp", axis=0, tiled=True)

    names = jnp.arange(EXPERTS, dtype=jnp.int32)[:, None]
    chosen = (routes[:, 0][None, :] == names) | (routes[:, 1][None, :] == names)
    by_sequence = chosen.reshape(EXPERTS * sequences, SEQ_LEN)
    order = jnp.arange(SEQ_LEN, dtype=jnp.int32)
    earlier = (order[:, None] < order[None, :]).astype(bf16)
    counts = dot(by_sequence.astype(bf16), earlier)
    places = jnp.where(by_sequence, counts, -1.0).reshape(EXPERTS, sequences, 2, local_rows)
    places = jnp.where(odd, places[:, :, ::-1], places)
    places = jnp.where(low, places, places[:, ::-1]).reshape(EXPERTS, sequences, SEQ_LEN)
    places = [places[:, s] for s in range(sequences)]

    sequence = ordered(tokens, token_partner)
    sequence, *places = lax.optimization_barrier((sequence, *places))
    if split:
        sequence, *crossed = lax.optimization_barrier((sequence, *crossed))
        seconds = [
            from_group(after(block, other), way[1])
            for block, other, way in zip(blocks, crossed, ways)
        ]
    out_near = spread_near(after(cotangent, token_partner))
    normed = norm_rows(sequence.astype(f32), attn_gain).astype(bf16)
    if split:
        normed, *seconds = lax.optimization_barrier((normed, *seconds))
        thirds = [
            from_group(after(other, second), way[1])
            for other, second, way in zip(crossed, seconds, ways)
        ]
    project = dot(normed, qkv_matrix).astype(bf16)
    router_t = router.T
    project, router_t, *near = lax.optimization_barrier((project, router_t) + out_near[1:])
    out_near = out_near[:1] + tuple(near)
    out_far = spread_far(out_near)
    context, log_totals = attend_forward(project)
    kept = lax.dynamic_slice_in_dim(context, half * local_rows, local_rows, 0)
    sent = lax.dynamic_slice_in_dim(context, (1 - half) * local_rows, local_rows, 0)
    context = jnp.concatenate([kept, from_partner(sent, 1)], axis=1)
    inputs = tokens.astype(f32)
    if split:
        context, *thirds = lax.optimization_barrier((context, *thirds))
        weights = [
            {0: block, one: first, two: second, one ^ two: third}
            for block, first, second, third, (one, two) in zip(
                blocks, crossed, seconds, thirds, ways
            )
        ]
    else:
        weights = [{0: lax.all_gather(block, "dp", axis=1, tiled=True)} for block in blocks]
    middle = inputs + dot(context, proj_matrix, NT)
    moe_normed = norm_rows(middle, moe_gain).astype(bf16)
    moe_near = lax.optimization_barrier(spread_near(moe_normed))
    expert_first, expert_second = (gathered(item) for item in weights)
    moe_far = spread_far(moe_near)

    place_info = jnp.stack([me, edge.astype(jnp.int32)]).astype(jnp.int32)
    run = lambda s, rows, upstream: through_experts(
        place_info, places[s], router_t, rows, upstream, expert_first, expert_second
    )
    halves = lambda near: [(item,) for item in near[:2]]
    own = run(0, halves(moe_near), halves(out_near))
    own_outs = expert_outputs(place_info, places[:1], [own[5]], expert_second)
    late = all_after(moe_far + out_far, own_outs[0])
    choices = lambda far: [far[:2], far[2:]]
    other = run(1, choices(late[:4]), choices(late[4:]))
    started = collect_start(other[0], other[1])
    line = lambda item, i: item[:, i * local_rows : (i + 1) * local_rows]
    parts = 8 if split else 1
    grads = expert_grads(place_info, [item[3:] for item in (own, other)], parts)
    activated = all_after([other[5]], grads[0])
    other_outs = expert_outputs(place_info, places[1:], activated, expert_second)
    started = all_after(started, other_outs[0])
    middle_back = collect_middle(other[1], started)
    collected = collect_end(own[0], own[1], started, middle_back, edge)
    moe_back, gate_grad = collected[:local_rows], collected[local_rows : local_rows + EXPERTS, :local_rows]
    outs = list(own_outs) + list(other_outs)
    if split:
        received = [from_group(grads[i], 1) for i in (1, 3)]
        received = all_after(received, other_outs[0])
        scattering = [
            scatter_start(me, grads[2 * i], received[i], way) for i, way in enumerate(ways)
        ]
        collected, *sent = lax.optimization_barrier((collected,) + tuple(item[1] for item in scattering))
        scattering = [(item[0], value) for item, value in zip(scattering, sent)]
        moe_back = collected[:local_rows]

    out_grad = cotangent.astype(f32)
    local_gates = line(own[2], 0)
    logit_grad = local_gates * (
        gate_grad - jnp.sum(local_gates * gate_grad, axis=0, keepdims=True)
    )
    logit_grad = logit_grad.astype(bf16)
    router_grad = dot(moe_normed, logit_grad, (((0,), (1,)), ((), ())))
    router_back = dot(logit_grad, router, (((0,), (1,)), ((), ())))
    middle_norm, moe_gain_grad = norm_back(middle, moe_gain, moe_back + router_back)
    middle_grad = out_grad + middle_norm
    attn_grad = middle_grad.astype(bf16)
    context_grad = dot(attn_grad, proj_matrix).astype(bf16)
    context_partner = from_partner(context_grad[:, side:], 1)
    context_grad = ordered(context_grad[:, :side], context_partner)
    if split:
        received = [from_group(item[1], way[0]) for item, way in zip(scattering, ways)]
    proj_grad = dot(attn_grad, context, TN)
    small_grad = jnp.concatenate([moe_gain_grad[:, None], router_grad], 1)
    small_grad = jnp.pad(small_grad, ((0, 0), (0, LANES - small_grad.shape[1])))
    early = jnp.concatenate([proj_grad, small_grad], axis=1).astype(bf16)
    early = lax.psum_scatter(early, "dp", scatter_dimension=0, tiled=True)
    project_grad = attend_backward(project, context_grad, log_totals)
    sent = lax.dynamic_slice_in_dim(project_grad, (1 - half) * local_rows, local_rows, 0)
    kept = lax.dynamic_slice_in_dim(project_grad, half * local_rows, local_rows, 0)
    arrived = from_partner(dot(sent, qkv_matrix, NT).astype(bf16), 1)
    attn_back = dot(kept, qkv_matrix, NT) + arrived.astype(f32)
    if split:
        attn_back, *received = lax.optimization_barrier((attn_back, *received))
        scattering = [
            scatter_step(me, item[0] + [value], 1, way[1])
            for item, value, way in zip(scattering, received, ways)
        ]
        received = [from_group(item[1], way[1]) for item, way in zip(scattering, ways)]
        first_total, second_total = (
            summed(item[0] + [value]) for item, value in zip(scattering, received)
        )
    else:
        first_total, second_total = (
            lax.psum_scatter(item[0][:, 0], "dp", scatter_dimension=1, tiled=True).astype(f32)
            for item in (grads[:1], grads[1:])
        )
    second_total = second_total.transpose(0, 2, 1)
    input_norm, attn_gain_grad = norm_back(inputs, attn_gain, attn_back)
    input_grad = middle_grad + input_norm
    qkv_grad = dot(normed, project_grad, TN)

    outs = all_after(outs, context_partner)
    started = all_after(collect_start(outs[2], outs[3]), project_grad)
    ended = collect_end(outs[0], outs[1], started, collect_middle(outs[3], started), edge)
    result = middle + ended

    qkv_late = lax.psum_scatter(
        qkv_grad.astype(bf16), "dp", scatter_dimension=0, tiled=True
    )
    gain_part = lax.psum_scatter(attn_gain_grad, "dp", scatter_dimension=0, tiled=True)
    proj_part = early[:, : 4 * quarter].reshape(depth, 4, quarter)
    small_part = early[:, 4 * quarter :].reshape(4, part, LANES)

    def message(distance):
        pieces = {0: (0, 1), 1: (2, 3), 2: (1, 0), 3: (3, 2)}[distance]
        proj_piece = jnp.where(low, proj_part[:, pieces[0]], proj_part[:, pieces[1]])
        small_piece = lax.dynamic_slice_in_dim(small_part, place_z ^ distance, 1, 0)[0]
        small_piece = jnp.pad(small_piece, ((0, depth - part), (0, 0)))
        return jnp.concatenate([proj_piece, small_piece], axis=1)

    shared = summed(
        [message(0)] + [from_partner(message(distance), distance) for distance in (1, 2, 3)]
    )
    proj_total = shared[:, :quarter].T
    small_total = shared[:part, quarter:]
    qkv_part = qkv_late.reshape(depth, 3, 2, quarter)
    gain_part = gain_part.reshape(4, part)
    gain_piece = lambda distance: lax.dynamic_slice_in_dim(gain_part, place_z ^ distance, 1, 0)[0]
    gain_total = summed(
        [gain_piece(0)] + [from_partner(gain_piece(distance), distance) for distance in (1, 2, 3)]
    )
    crossing = jnp.where(low, qkv_part[:, :, 1], qkv_part[:, :, 0])
    qkv_total = jnp.where(low, qkv_part[:, :, 0], qkv_part[:, :, 1]).astype(f32)
    qkv_total = qkv_total + from_partner(crossing.reshape(depth, 3 * quarter), 2).astype(
        f32
    ).reshape(depth, 3, quarter)
    return (
        result,
        input_grad,
        gain_total,
        small_total[:, 0],
        small_total[:, 1 : 1 + EXPERTS],
        qkv_total,
        proj_total,
        first_total,
        second_total,
    )


def solution(mesh):
    in_specs = (
        P(("dp", "tensor"), None),
        P(("dp", "tensor"), None),
        P("dp", None),
        P(("dp", "tensor")),
        P(("dp", "tensor")),
        P(("dp", "tensor"), None),
        P("dp", None, "tensor"),
        P("tensor", "dp"),
        P(None, "dp", "tensor"),
        P(None, "tensor", "dp"),
    )
    out_specs = (
        P(("dp", "tensor"), None),
        P(("dp", "tensor"), None),
        P(("dp", "tensor")),
        P(("dp", "tensor")),
        P(("dp", "tensor"), None),
        P("dp", None, "tensor"),
        P("tensor", "dp"),
        P(None, "dp", "tensor"),
        P(None, "tensor", "dp"),
    )
    return jax.shard_map(shards, mesh=mesh, in_specs=in_specs, out_specs=out_specs, check_vma=False)
```

```python
import functools

import jax
import jax.numpy as jnp
from jax import lax
from jax.experimental import pallas as pl
from jax.experimental.pallas import tpu as pltpu
from jax.sharding import PartitionSpec as P

DH = 64
EXPERTS = 8
SEQ_LEN = 1024
CAP = 320
BLOCK = 256
LANES = 128

epsilon = 1e-06
masked_score = -1e30
vmem_bytes = 56 * 1024 * 1024

f32 = jnp.float32
bf16 = jnp.bfloat16
NT = (((1,), (1,)), ((), ()))
TN = (((0,), (0,)), ((), ()))


def norm_rows(series, scales):
    return series * lax.rsqrt(jnp.mean(series * series, axis=-1, keepdims=True) + epsilon) * scales


def norm_back(series, scales, upstream):
    factor = lax.rsqrt(jnp.mean(series * series, axis=-1, keepdims=True) + epsilon)
    normed = series * factor
    scaled = upstream * scales
    series_grad = factor * (scaled - normed * jnp.mean(scaled * normed, axis=-1, keepdims=True))
    return (series_grad, jnp.sum(upstream * normed, axis=0))


def dot(a, b, dims=None):
    if dims is None:
        dims = (((1,), (0,)), ((), ()))
    return lax.dot_general(a, b, dims, preferred_element_type=f32)


def head_masks(scale):
    lane = lax.broadcasted_iota(jnp.int32, (1, LANES), 1)
    return [
        jnp.where((lane >= head * DH) & (lane < (head + 1) * DH), scale, 0.0).astype(bf16)
        for head in range(LANES // DH)
    ]


def causal_block():
    shape = (BLOCK, BLOCK)
    return lax.broadcasted_iota(jnp.int32, shape, 0) <= lax.broadcasted_iota(jnp.int32, shape, 1)


def attend_forward_kernel(query, keys, values, context, log_totals):
    masks = head_masks(DH**-0.5)
    seen = causal_block()
    values_t = values[...].astype(f32).T.astype(bf16)
    for i in range(SEQ_LEN // BLOCK):
        rows = slice(i * BLOCK, (i + 1) * BLOCK)
        parts = []
        for head, mask in enumerate(masks):
            piece = query[rows, :] * mask
            scores = [
                dot(keys[j * BLOCK : (j + 1) * BLOCK, :], piece, NT) for j in range(i + 1)
            ]
            scores[i] = jnp.where(seen, scores[i], masked_score)
            largest = jnp.max(scores[0], axis=0, keepdims=True)
            for block in scores[1:]:
                largest = jnp.maximum(largest, jnp.max(block, axis=0, keepdims=True))
            raised = [jnp.exp(block - largest) for block in scores]
            total = jnp.sum(raised[0], axis=0, keepdims=True)
            for block in raised[1:]:
                total = total + jnp.sum(block, axis=0, keepdims=True)
            summed = dot(
                values_t[head * DH : (head + 1) * DH, : (i + 1) * BLOCK],
                jnp.concatenate([block.astype(bf16) for block in raised], axis=0),
            )
            parts.append(summed / total)
            log_totals[0, head : head + 1, rows] = largest + jnp.log(total)
        context[rows, :] = jnp.concatenate(parts, axis=0).T.astype(bf16)


def attend_forward(project):
    pairs = project.shape[1] // (3 * LANES)
    column = lambda c: pl.BlockSpec((SEQ_LEN, LANES), lambda g, c=c: (0, c * pairs + g))
    heads = LANES // DH
    return pl.pallas_call(
        attend_forward_kernel,
        grid=(pairs,),
        in_specs=[column(0), column(1), column(2)],
        out_specs=[
            pl.BlockSpec((SEQ_LEN, LANES), lambda g: (0, g)),
            pl.BlockSpec((1, heads, SEQ_LEN), lambda g: (g, 0, 0)),
        ],
        out_shape=[
            jax.ShapeDtypeStruct((SEQ_LEN, pairs * LANES), bf16),
            jax.ShapeDtypeStruct((pairs, heads, SEQ_LEN), f32),
        ],
        compiler_params=pltpu.CompilerParams(vmem_limit_bytes=vmem_bytes),
        cost_estimate=estimate(14 << 30, 4 << 20),
        name="attend_forward",
    )(project, project, project)


def attend_backward_kernel(pairs, query, keys, values, upstream, log_totals, grads, key_sum, value_sum):
    g = pl.program_id(0)
    scaled_masks = head_masks(DH**-0.5)
    masks = head_masks(1.0)
    seen = causal_block()
    keys_t = keys[...].astype(f32).T.astype(bf16)
    key_sum[...] = jnp.zeros_like(key_sum)
    value_sum[...] = jnp.zeros_like(value_sum)
    for i in range(SEQ_LEN // BLOCK):
        rows = slice(i * BLOCK, (i + 1) * BLOCK)
        parts = []
        for head in range(LANES // DH):
            piece = query[rows, :] * scaled_masks[head]
            above = upstream[rows, :] * masks[head]
            log_total = log_totals[0, head : head + 1, rows]
            weights, probs = [], []
            inner = jnp.zeros((1, BLOCK), f32)
            for j in range(i + 1):
                columns = slice(j * BLOCK, (j + 1) * BLOCK)
                scores = dot(keys[columns, :], piece, NT)
                if j == i:
                    scores = jnp.where(seen, scores, masked_score)
                weights.append(jnp.exp(scores - log_total))
                probs.append(dot(values[columns, :], above, NT))
                inner = inner + jnp.sum(weights[j] * probs[j], axis=0, keepdims=True)
            score_grads = []
            for j in range(i + 1):
                score_grads.append((weights[j] * (probs[j] - inner)).astype(bf16))
            length = (i + 1) * BLOCK
            all_grads = jnp.concatenate(score_grads, axis=0)
            all_weights = jnp.concatenate([block.astype(bf16) for block in weights], axis=0)
            value_sum[:length, :] += dot(all_weights, above)
            key_sum[:length, :] += dot(all_grads, piece)
            parts.append(dot(keys_t[head * DH : (head + 1) * DH, :length], all_grads))
        query_grad = jnp.concatenate(parts, axis=0).T * DH**-0.5
        grads[rows, pl.ds(pl.multiple_of(g * LANES, LANES), LANES)] = query_grad.astype(bf16)
    grads[:, pl.ds(pl.multiple_of((pairs + g) * LANES, LANES), LANES)] = key_sum[...].astype(bf16)
    grads[:, pl.ds(pl.multiple_of((2 * pairs + g) * LANES, LANES), LANES)] = value_sum[...].astype(
        bf16
    )


def attend_backward(project, upstream, log_totals):
    pairs = project.shape[1] // (3 * LANES)
    column = lambda c: pl.BlockSpec((SEQ_LEN, LANES), lambda g, c=c: (0, c * pairs + g))
    heads = LANES // DH
    return pl.pallas_call(
        functools.partial(attend_backward_kernel, pairs),
        grid=(pairs,),
        in_specs=[
            column(0),
            column(1),
            column(2),
            column(0),
            pl.BlockSpec((1, heads, SEQ_LEN), lambda g: (g, 0, 0)),
        ],
        out_specs=pl.BlockSpec(project.shape, lambda g: (0, 0)),
        out_shape=jax.ShapeDtypeStruct(project.shape, bf16),
        scratch_shapes=[pltpu.VMEM((SEQ_LEN, LANES), f32), pltpu.VMEM((SEQ_LEN, LANES), f32)],
        compiler_params=pltpu.CompilerParams(vmem_limit_bytes=vmem_bytes),
        cost_estimate=estimate(20 << 30, 8 << 20),
        name="attend_backward",
    )(project, project, project, upstream, log_totals)


def slot_hits(place):
    return lax.broadcasted_iota(jnp.int32, (CAP, SEQ_LEN), 0) == place.astype(jnp.int32)


GROUP = 4


def keep_term(expert, onehots, terms, onehot, term):
    rows = pl.ds(pl.multiple_of(expert % GROUP * CAP, 64), CAP)
    onehots[rows, :] = onehot
    terms[rows, :] = term


def add_terms(expert, onehots, terms, total, results):
    @pl.when(expert % GROUP == GROUP - 1)
    def _():
        for i in range(SEQ_LEN // BLOCK):
            rows = slice(i * BLOCK, (i + 1) * BLOCK)
            term = dot(onehots[:, rows], terms[...], TN)

            @pl.when(expert == GROUP - 1)
            def _():
                total[rows, :] = term

            @pl.when(expert == EXPERTS - 1)
            def _():
                result = results[i // (SEQ_LEN // BLOCK // 2)]
                first = i % (SEQ_LEN // BLOCK // 2) * BLOCK
                result[first : first + BLOCK, :] = (total[rows, :] + term).astype(bf16)


def combine_scratch(width):
    return [
        pltpu.VMEM((GROUP * CAP, SEQ_LEN), bf16),
        pltpu.VMEM((GROUP * CAP, width), bf16),
        pltpu.VMEM((SEQ_LEN, width), f32),
    ]


def assemble(me, offsets, blocks, weight):
    rows = weight.shape[0] // len(offsets)
    for i, offset in enumerate(offsets):
        start = 0 if len(offsets) == 1 else pl.multiple_of((me ^ offset) * rows, 16)
        weight[pl.ds(start, rows), :] = blocks[i][0]


def fill(edge, parts, whole):
    rows = SEQ_LEN // 2
    for i, choices in enumerate(parts):
        target = slice(i * rows, (i + 1) * rows)
        if len(choices) == 1:
            whole[target, :] = choices[0][...]
            continue

        @pl.when(edge == 1)
        def _():
            whole[target, :] = choices[0][...]

        @pl.when(edge == 0)
        def _():
            whole[target, :] = choices[1][...]


def expert_kernel(offsets, choices, place_info, place, router, *refs):
    count = len(offsets[0])
    groups = []
    for _ in range(4):
        groups.append(refs[:choices])
        refs = refs[choices:]
    first_blocks, second_blocks = refs[:count], refs[count : 2 * count]
    back, back_two, gates, slots_in, slots_grad, activated, hidden_grad = refs[
        2 * count : 2 * count + 7
    ]
    onehots, terms, total, first, second, gate_grad, rows, upstream = refs[2 * count + 7 :]
    expert = pl.program_id(0)
    assemble(place_info[0], offsets[0], first_blocks, first)
    assemble(place_info[0], offsets[1], second_blocks, second)

    @pl.when(expert == 0)
    def _():
        fill(place_info[1], groups[:2], rows)
        fill(place_info[1], groups[2:], upstream)
        logits = dot(router[...], rows[...], NT)
        chosen = place[...] >= 0.0
        largest = jnp.max(jnp.where(chosen, logits, masked_score), axis=0, keepdims=True)
        raised = jnp.where(chosen, jnp.exp(jnp.where(chosen, logits - largest, 0.0)), 0.0)
        gates[...] = raised / jnp.sum(raised, axis=0, keepdims=True)

    row = pl.ds(expert, 1)
    hits = slot_hits(place[row, :])
    onehot = jnp.where(hits, 1.0, 0.0).astype(bf16)
    entered = dot(onehot, rows[...]).astype(bf16)
    above = dot(onehot, upstream[...]).astype(bf16)
    slot_gate = jnp.sum(jnp.where(hits, gates[row, :], 0.0), axis=1, keepdims=True)
    hidden = dot(entered, first[...])
    raw_grad = dot(above, second[...])
    slots_in[0] = entered
    slots_grad[0] = above
    square = hidden * hidden
    factor = 0.7978845608028654
    bent = jnp.tanh(factor * hidden * (1.0 + 0.044715 * square))
    half = 0.5 * (1.0 + bent)
    active = (hidden * half).astype(bf16)
    slope = half + 0.5 * hidden * (1.0 - bent * bent) * (factor * (1.0 + 3 * 0.044715 * square))
    activated[0] = (slot_gate * active.astype(f32)).astype(bf16)
    slot_gate_grad = jnp.sum(active.astype(f32) * raw_grad, axis=1, keepdims=True)
    gate_grad[row, :] = jnp.sum(jnp.where(hits, slot_gate_grad, 0.0), axis=0, keepdims=True)
    below = (slot_gate * raw_grad * slope).astype(bf16)
    hidden_grad[0] = below
    slot_back = dot(below, first[...], NT).astype(bf16)
    keep_term(expert, onehots, terms, onehot, slot_back)
    add_terms(expert, onehots, terms, total, (back, back_two))

    @pl.when(expert == EXPERTS - 1)
    def _():
        half = SEQ_LEN // 2
        for i, result in enumerate((back, back_two)):
            result[half:, :] = jnp.zeros((result.shape[0] - half, result.shape[1]), bf16)
            grads = gate_grad[:, i * half : (i + 1) * half]
            result[half:, :half] = jnp.concatenate([grads, jnp.zeros_like(grads)], 0).astype(bf16)


def block_specs(blocks):
    return [pl.BlockSpec((1,) + block.shape[1:], lambda e: (e, 0, 0)) for block in blocks]


def estimate(flops, moved):
    return pl.CostEstimate(flops=flops, bytes_accessed=moved, transcendentals=0)


scalar = pl.BlockSpec(memory_space=pltpu.SMEM)


def through_experts(place_info, place, router, row_parts, upstream_parts, first, second):
    parts = row_parts + upstream_parts
    choices = len(parts[0])
    half, width = parts[0][0].shape
    hidden_width = first[1][0].shape[2]
    line = pl.BlockSpec((EXPERTS, SEQ_LEN), lambda e: (0, 0))
    whole = pl.BlockSpec((half, width), lambda e: (0, 0))
    under = pl.BlockSpec((half + 16, width), lambda e: (0, 0))
    slots = lambda columns: pl.BlockSpec((1, CAP, columns), lambda e: (e, 0, 0))
    slot_shape = lambda columns: jax.ShapeDtypeStruct((EXPERTS, CAP, columns), bf16)
    return pl.pallas_call(
        functools.partial(expert_kernel, (first[0], second[0]), choices),
        grid=(EXPERTS,),
        in_specs=[scalar, line, pl.BlockSpec((EXPERTS, width), lambda e: (0, 0))]
        + [whole] * (4 * choices)
        + block_specs(first[1])
        + block_specs(second[1]),
        out_specs=[
            under,
            under,
            line,
            slots(width),
            slots(width),
            slots(hidden_width),
            slots(hidden_width),
        ],
        out_shape=[
            jax.ShapeDtypeStruct((half + 16, width), bf16),
            jax.ShapeDtypeStruct((half + 16, width), bf16),
            jax.ShapeDtypeStruct((EXPERTS, SEQ_LEN), f32),
            slot_shape(width),
            slot_shape(width),
            slot_shape(hidden_width),
            slot_shape(hidden_width),
        ],
        scratch_shapes=combine_scratch(width)
        + [
            pltpu.VMEM((width, hidden_width), bf16),
            pltpu.VMEM((width, hidden_width), bf16),
            pltpu.VMEM((EXPERTS, SEQ_LEN), f32),
            pltpu.VMEM((SEQ_LEN, width), bf16),
            pltpu.VMEM((SEQ_LEN, width), bf16),
        ],
        compiler_params=pltpu.CompilerParams(vmem_limit_bytes=vmem_bytes),
        cost_estimate=estimate(60 << 30, 50 << 20),
        name="through_experts",
    )(place_info, place, router, *[item for part in parts for item in part], *first[1], *second[1])


def grads_kernel(count, parts, place_info, *refs):
    slots_in, slots_grad, activated, hidden_grad = [
        jnp.concatenate([ref[0] for ref in refs[i * count : (i + 1) * count]], axis=0)
        for i in range(4)
    ]
    outs = refs[4 * count :]
    even = (place_info[0] & 1) == 0
    for i, (left, right) in enumerate(((slots_in, hidden_grad), (slots_grad, activated))):
        product = dot(left, right, TN)
        if parts == 1:
            outs[i][0, 0] = product.astype(bf16)
            continue
        rows = product.shape[0] // parts
        for j in range(parts // 2):
            one = product[2 * j * rows : (2 * j + 1) * rows]
            two = product[(2 * j + 1) * rows : (2 * j + 2) * rows]
            outs[2 * i][0, j] = jnp.where(even, one, two).astype(bf16)
            outs[2 * i + 1][0, j] = jnp.where(even, two, one).astype(bf16)


def expert_grads(place_info, sequences, parts):
    count = len(sequences)
    width, hidden_width = sequences[0][0].shape[2], sequences[0][2].shape[2]
    slots = lambda columns: pl.BlockSpec((1, CAP, columns), lambda e: (e, 0, 0))
    specs = [slots(width), slots(width), slots(hidden_width), slots(hidden_width)]
    shape = (max(parts // 2, 1), width // parts, hidden_width)
    outs = 2 * min(parts, 2)
    return pl.pallas_call(
        functools.partial(grads_kernel, count, parts),
        grid=(EXPERTS,),
        in_specs=[scalar] + [spec for spec in specs for _ in range(count)],
        out_specs=[pl.BlockSpec((1,) + shape, lambda e: (e, 0, 0, 0))] * outs,
        out_shape=[jax.ShapeDtypeStruct((EXPERTS,) + shape, bf16)] * outs,
        compiler_params=pltpu.CompilerParams(vmem_limit_bytes=vmem_bytes),
        cost_estimate=estimate(50 << 30, 50 << 20),
        name="expert_grads",
    )(place_info, *[item[i] for i in range(4) for item in sequences])


def outputs_kernel(count, offsets, place_info, *refs):
    expert = pl.program_id(0)
    blocks_count = len(offsets)
    place, activated = refs[:count], refs[count : 2 * count]
    blocks = refs[2 * count : 2 * count + blocks_count]
    refs = refs[2 * count + blocks_count :]
    second = refs[-1]
    assemble(place_info[0], offsets, blocks, second)
    for s in range(count):
        hits = slot_hits(place[s][pl.ds(expert, 1), :])
        out = dot(activated[s][0], second[...], NT).astype(bf16)
        onehot = jnp.where(hits, 1.0, 0.0).astype(bf16)
        onehots, terms, total = refs[2 * count + 3 * s : 2 * count + 3 * s + 3]
        keep_term(expert, onehots, terms, onehot, out)
        add_terms(expert, onehots, terms, total, refs[2 * s : 2 * s + 2])


def expert_outputs(place_info, places, activated, second):
    count = len(places)
    hidden_width = second[1][0].shape[2]
    width = second[1][0].shape[1] * len(second[0])
    half = SEQ_LEN // 2
    line = pl.BlockSpec((EXPERTS, SEQ_LEN), lambda e: (0, 0))
    whole = pl.BlockSpec((half, width), lambda e: (0, 0))
    slots = pl.BlockSpec((1, CAP, hidden_width), lambda e: (e, 0, 0))
    return pl.pallas_call(
        functools.partial(outputs_kernel, count, second[0]),
        grid=(EXPERTS,),
        in_specs=[scalar] + [line] * count + [slots] * count + block_specs(second[1]),
        out_specs=[whole] * (2 * count),
        out_shape=[jax.ShapeDtypeStruct((half, width), bf16)] * (2 * count),
        scratch_shapes=combine_scratch(width) * count + [pltpu.VMEM((width, hidden_width), bf16)],
        compiler_params=pltpu.CompilerParams(vmem_limit_bytes=vmem_bytes),
        cost_estimate=estimate(60 << 30, 30 << 20),
        name="expert_outputs",
    )(place_info, *places, *activated, *second[1])


def from_partner(value, distance):
    return lax.ppermute(value, "tensor", [(i, i ^ distance) for i in range(4)])


def between(value, *pairs):
    return lax.ppermute(value, "tensor", list(pairs))


def from_group(value, distance):
    count = lax.axis_size("dp")
    return lax.ppermute(value, "dp", [(i, i ^ distance) for i in range(count)])


def after(value, *others):
    return lax.optimization_barrier((value,) + others)[0]


def all_after(values, *others):
    return lax.optimization_barrier(tuple(values) + others)[: len(values)]


def summed(items):
    total = items[0].astype(f32)
    for item in items[1:]:
        total = total + item.astype(f32)
    return total


def spread_near(mine):
    return (mine, from_partner(mine, 1), between(mine, (1, 2), (2, 1)))


def spread_far(near):
    mine, partner, middle = near
    far = between(after(mine, partner, middle), (0, 3), (3, 0))
    return (
        between(middle, (1, 0), (2, 3)),
        between(partner, (1, 2), (2, 1)),
        far,
        middle,
    )


def collect_start(two, three):
    far = between(three, (0, 3), (3, 0))
    inward = between(two, (0, 1), (3, 2))
    across = between(two, (1, 2), (2, 1))
    return far, inward, across


def collect_middle(three, started):
    return between(summed([three, started[1]]).astype(bf16), (1, 2), (2, 1))


def collect_end(mine, partner, started, middle, edge, waits=()):
    far, _, across = started
    partner = jnp.where(edge, partner, summed([partner, across]).astype(bf16))
    received, middle = all_after([from_partner(partner, 1), middle], *waits)
    return summed([mine, received, jnp.where(edge, far, middle)])


def grouped(block):
    return lax.axis_size("dp") == 8 and block.shape[1] % 16 == 0


def gathered(blocks):
    if len(blocks) > 1:
        blocks.update({offset ^ 1: from_group(item, 1) for offset, item in list(blocks.items())})
    return (tuple(blocks), list(blocks.values()))


def scatter_step(me, items, axis, distance):
    bit = (me // distance) & 1
    take = lambda item, which: lax.dynamic_index_in_dim(item, which, axis, keepdims=False)
    sent = summed([take(item, 1 - bit) for item in items]).astype(bf16)
    return [take(item, bit) for item in items], sent


def scatter_start(me, kept, received, way):
    items = [item.reshape((EXPERTS, 2, 2) + item.shape[2:]) for item in (kept, received)]
    return scatter_step(me, items, 1 if way[0] == 4 else 2, way[0])


def shards(
    tokens,
    cotangent,
    routes,
    gain_attention,
    gain_experts,
    router_weight,
    qkv_weight,
    proj_weight,
    expert_in,
    expert_back,
):
    local_rows, width = tokens.shape
    group_rows = routes.shape[0]
    sequences = group_rows // SEQ_LEN
    depth, _, quarter = qkv_weight.shape
    part = depth // 4
    side = 2 * quarter
    place_z = lax.axis_index("tensor")
    me = lax.axis_index("dp")
    odd = (place_z & 1) == 1
    low = place_z < 2
    half = place_z & 1
    edge = (place_z == 0) | (place_z == 3)

    def ordered(mine, other):
        return jnp.where(
            odd,
            jnp.concatenate([other, mine], axis=0),
            jnp.concatenate([mine, other], axis=0),
        )

    small = jnp.concatenate([gain_attention[:, None], gain_experts[:, None], router_weight], axis=1)
    small = jnp.pad(small, ((0, depth - part), (0, LANES - small.shape[1])))
    mine = qkv_weight.reshape(depth, 3 * quarter)
    small = small[:part]
    across = from_partner(mine, 2)
    smalls = [small] + [from_partner(small, distance) for distance in (1, 2, 3)]
    pick = lambda items: (
        jnp.where(low, items[0], items[2]),
        jnp.where(low, items[2], items[0]),
        jnp.where(low, items[1], items[3]),
        jnp.where(low, items[3], items[1]),
    )
    smalls = pick(smalls)
    smalls = jnp.where(
        odd,
        jnp.concatenate([smalls[2], smalls[0], smalls[3], smalls[1]], axis=0),
        jnp.concatenate([smalls[0], smalls[2], smalls[1], smalls[3]], axis=0),
    )
    one = jnp.where(low, mine, across).reshape(depth, 3, quarter)
    two = jnp.where(low, across, mine).reshape(depth, 3, quarter)
    packed = jnp.concatenate(
        [jnp.concatenate([one, two], axis=2).reshape(depth, 3 * side), smalls], axis=1
    )
    ways = ((2, 4), (4, 2))
    blocks = [expert_in, expert_back.transpose(0, 2, 1)]
    split = grouped(blocks[0])
    if split:
        crossed = [from_group(block, way[0]) for block, way in zip(blocks, ways)]
    packed = lax.all_gather(packed, "dp", axis=0, tiled=True)
    qkv_matrix = packed[:, : 3 * side]
    small = packed[:, 3 * side :]
    attn_gain = small[:, 0].astype(f32)
    moe_gain = small[:, 1].astype(f32)
    router = small[:, 2 : 2 + EXPERTS]
    token_partner = from_partner(after(tokens, across), 1)
    projection = after(proj_weight.T, token_partner)
    projections = [projection] + [from_partner(projection, distance) for distance in (1, 2, 3)]
    proj_matrix = jnp.concatenate(pick(projections), axis=1)
    proj_matrix = lax.all_gather(proj_matrix, "dp", axis=0, tiled=True)

    names = jnp.arange(EXPERTS, dtype=jnp.int32)[:, None]
    chosen = (routes[:, 0][None, :] == names) | (routes[:, 1][None, :] == names)
    by_sequence = chosen.reshape(EXPERTS * sequences, SEQ_LEN)
    order = jnp.arange(SEQ_LEN, dtype=jnp.int32)
    earlier = (order[:, None] < order[None, :]).astype(bf16)
    counts = dot(by_sequence.astype(bf16), earlier)
    places = jnp.where(by_sequence, counts, -1.0).reshape(EXPERTS, sequences, 2, local_rows)
    places = jnp.where(odd, places[:, :, ::-1], places)
    places = jnp.where(low, places, places[:, ::-1]).reshape(EXPERTS, sequences, SEQ_LEN)
    places = [places[:, s] for s in range(sequences)]

    sequence = ordered(tokens, token_partner)
    sequence, *places = lax.optimization_barrier((sequence, *places))
    if split:
        sequence, *crossed = lax.optimization_barrier((sequence, *crossed))
        seconds = [
            from_group(after(block, other), way[1])
            for block, other, way in zip(blocks, crossed, ways)
        ]
    out_near = spread_near(after(cotangent, token_partner))
    normed = norm_rows(sequence.astype(f32), attn_gain).astype(bf16)
    project = dot(normed, qkv_matrix).astype(bf16)
    router_t = router.T
    project, router_t, *near = lax.optimization_barrier((project, router_t) + out_near[1:])
    out_near = out_near[:1] + tuple(near)
    out_far = spread_far(out_near)
    context, log_totals = attend_forward(project)
    if split:
        context, *seconds = lax.optimization_barrier((context, *seconds))
        thirds = [
            from_group(after(other, second), way[1])
            for other, second, way in zip(crossed, seconds, ways)
        ]
    kept = lax.dynamic_slice_in_dim(context, half * local_rows, local_rows, 0)
    sent = lax.dynamic_slice_in_dim(context, (1 - half) * local_rows, local_rows, 0)
    context = jnp.concatenate([kept, from_partner(sent, 1)], axis=1)
    inputs = tokens.astype(f32)
    middle = inputs + dot(context, proj_matrix, NT)
    moe_normed = norm_rows(middle, moe_gain).astype(bf16)
    moe_near = lax.optimization_barrier(
        spread_near(moe_normed) + (tuple(thirds) if split else ())
    )
    moe_near, thirds = moe_near[:3], moe_near[3:]
    if split:
        weights = [
            {0: block, one: first, two: second, one ^ two: third}
            for block, first, second, third, (one, two) in zip(
                blocks, crossed, seconds, thirds, ways
            )
        ]
    else:
        weights = [{0: lax.all_gather(block, "dp", axis=1, tiled=True)} for block in blocks]
    expert_first, expert_second = (gathered(item) for item in weights)
    moe_far = spread_far(moe_near)

    place_info = jnp.stack([me, edge.astype(jnp.int32)]).astype(jnp.int32)
    run = lambda s, rows, upstream: through_experts(
        place_info, places[s], router_t, rows, upstream, expert_first, expert_second
    )
    halves = lambda near: [(item,) for item in near[:2]]
    own = run(0, halves(moe_near), halves(out_near))
    own_outs = expert_outputs(place_info, places[:1], [own[5]], expert_second)
    late = all_after(moe_far + out_far, own_outs[0])
    choices = lambda far: [far[:2], far[2:]]
    other = run(1, choices(late[:4]), choices(late[4:]))
    started = collect_start(other[0], other[1])
    line = lambda item, i: item[:, i * local_rows : (i + 1) * local_rows]
    parts = 8 if split else 1
    grads = expert_grads(place_info, [item[3:] for item in (own, other)], parts)
    activated = all_after([other[5]], grads[0])
    other_outs = expert_outputs(place_info, places[1:], activated, expert_second)
    started = all_after(started, other_outs[0])
    middle_back = collect_middle(other[1], started)
    outs = list(own_outs) + list(other_outs)
    waits = ()
    if split:
        received = [from_group(grads[i], 1) for i in (1, 3)]
        received = all_after(received, other_outs[0])
        scattering = [
            scatter_start(me, grads[2 * i], received[i], way) for i, way in enumerate(ways)
        ]
        waits = lax.optimization_barrier(tuple(item[1] for item in scattering))
        scattering = [(item[0], value) for item, value in zip(scattering, waits)]
    collected = collect_end(own[0], own[1], started, middle_back, edge, waits)
    moe_back, gate_grad = collected[:local_rows], collected[local_rows : local_rows + EXPERTS, :local_rows]

    out_grad = cotangent.astype(f32)
    local_gates = line(own[2], 0)
    logit_grad = local_gates * (
        gate_grad - jnp.sum(local_gates * gate_grad, axis=0, keepdims=True)
    )
    logit_grad = logit_grad.astype(bf16)
    router_grad = dot(moe_normed, logit_grad, (((0,), (1,)), ((), ())))
    router_back = dot(logit_grad, router, (((0,), (1,)), ((), ())))
    middle_norm, moe_gain_grad = norm_back(middle, moe_gain, moe_back + router_back)
    middle_grad = out_grad + middle_norm
    attn_grad = middle_grad.astype(bf16)
    context_grad = dot(attn_grad, proj_matrix).astype(bf16)
    context_partner = from_partner(context_grad[:, side:], 1)
    context_grad = ordered(context_grad[:, :side], context_partner)
    if split:
        received = [from_group(item[1], way[0]) for item, way in zip(scattering, ways)]
    proj_grad = dot(attn_grad, context, TN)
    project_grad = attend_backward(project, context_grad, log_totals)
    sent = lax.dynamic_slice_in_dim(project_grad, (1 - half) * local_rows, local_rows, 0)
    kept = lax.dynamic_slice_in_dim(project_grad, half * local_rows, local_rows, 0)
    qkv_grad = dot(normed, project_grad, TN)
    outs = all_after(outs, context_partner)
    started = collect_start(outs[2], outs[3])
    if split:
        qkv_grad, *started = lax.optimization_barrier((qkv_grad, *started, *received))
        started, received = started[:3], started[3:]
    arrived = from_partner(dot(sent, qkv_matrix, NT).astype(bf16), 1)
    if split:
        scattering = [
            scatter_step(me, item[0] + [value], 1, way[1])
            for item, value, way in zip(scattering, received, ways)
        ]
        arrived, *sent = lax.optimization_barrier(
            (arrived,) + tuple(item[1] for item in scattering)
        )
    attn_back = dot(kept, qkv_matrix, NT) + arrived.astype(f32)
    if split:
        received = [from_group(item, way[1]) for item, way in zip(sent, ways)]
        kept_sums = all_after([summed(item[0]) for item in scattering], attn_back)
        first_total, second_total = (
            kept + value.astype(f32) for kept, value in zip(kept_sums, received)
        )
    else:
        first_total, second_total = (
            lax.psum_scatter(item[0][:, 0], "dp", scatter_dimension=1, tiled=True).astype(f32)
            for item in (grads[:1], grads[1:])
        )
    second_total = second_total.transpose(0, 2, 1)
    input_norm, _ = norm_back(inputs, attn_gain, attn_back)
    input_grad = middle_grad + input_norm

    scaled_gain_grad = jnp.sum(qkv_grad * qkv_matrix.astype(f32), axis=1, keepdims=True)
    small_grad = jnp.concatenate([scaled_gain_grad, moe_gain_grad[:, None], router_grad], 1)
    small_grad = jnp.pad(small_grad, ((0, 0), (0, LANES - small_grad.shape[1])))
    summed_late = lax.psum_scatter(
        jnp.concatenate([qkv_grad, proj_grad, small_grad], axis=1).astype(bf16),
        "dp",
        scatter_dimension=0,
        tiled=True,
    )

    waits = tuple(received) if split else ()
    ended = collect_end(outs[0], outs[1], started, collect_middle(outs[3], started), edge, waits)
    result = middle + ended

    qkv_part = summed_late[:, : 3 * side].reshape(depth, 3, 2, quarter)
    proj_part = summed_late[:, 3 * side : 3 * side + 4 * quarter].reshape(depth, 4, quarter)
    small_part = summed_late[:, 3 * side + 4 * quarter :].reshape(4, part, LANES)

    def message(distance):
        pieces = {0: (0, 1), 1: (2, 3), 2: (1, 0), 3: (3, 2)}[distance]
        proj_piece = jnp.where(low, proj_part[:, pieces[0]], proj_part[:, pieces[1]])
        small_piece = lax.dynamic_slice_in_dim(small_part, place_z ^ distance, 1, 0)[0]
        small_piece = jnp.pad(small_piece, ((0, depth - part), (0, 0)))
        items = [proj_piece, small_piece]
        if distance in (0, 2):
            qkv_piece = jnp.where(low, qkv_part[:, :, pieces[0]], qkv_part[:, :, pieces[1]])
            items.append(qkv_piece.reshape(depth, 3 * quarter))
        return jnp.concatenate(items, axis=1)

    total = summed([message(0), from_partner(message(2), 2)])
    split_at = quarter + LANES
    shared = summed(
        [total[:, :split_at]] + [from_partner(message(distance), distance) for distance in (1, 3)]
    )
    qkv_total = total[:, split_at:].reshape(depth, 3, quarter)
    proj_total = shared[:, :quarter].T
    small_total = shared[:part, quarter:]
    gain_total = small_total[:, 0] / gain_attention.astype(f32)
    return (
        result,
        input_grad,
        gain_total,
        small_total[:, 1],
        small_total[:, 2 : 2 + EXPERTS],
        qkv_total,
        proj_total,
        first_total,
        second_total,
    )


def solution(mesh):
    in_specs = (
        P(("dp", "tensor"), None),
        P(("dp", "tensor"), None),
        P("dp", None),
        P(("dp", "tensor")),
        P(("dp", "tensor")),
        P(("dp", "tensor"), None),
        P("dp", None, "tensor"),
        P("tensor", "dp"),
        P(None, "dp", "tensor"),
        P(None, "tensor", "dp"),
    )
    out_specs = (
        P(("dp", "tensor"), None),
        P(("dp", "tensor"), None),
        P(("dp", "tensor")),
        P(("dp", "tensor")),
        P(("dp", "tensor"), None),
        P("dp", None, "tensor"),
        P("tensor", "dp"),
        P(None, "dp", "tensor"),
        P(None, "tensor", "dp"),
    )
    return jax.shard_map(shards, mesh=mesh, in_specs=in_specs, out_specs=out_specs, check_vma=False)
```

```python
import functools

import jax
import jax.numpy as jnp
from jax import lax
from jax.experimental import pallas as pl
from jax.experimental.pallas import tpu as pltpu
from jax.sharding import PartitionSpec as P

DH = 64
EXPERTS = 8
SEQ_LEN = 1024
CAP = 320
BLOCK = 256
LANES = 128

epsilon = 1e-06
masked_score = -1e30
vmem_bytes = 56 * 1024 * 1024

f32 = jnp.float32
bf16 = jnp.bfloat16
NT = (((1,), (1,)), ((), ()))
TN = (((0,), (0,)), ((), ()))


def norm_rows(series, scales):
    return series * lax.rsqrt(jnp.mean(series * series, axis=-1, keepdims=True) + epsilon) * scales


def norm_back(series, scales, upstream):
    factor = lax.rsqrt(jnp.mean(series * series, axis=-1, keepdims=True) + epsilon)
    normed = series * factor
    scaled = upstream * scales
    series_grad = factor * (scaled - normed * jnp.mean(scaled * normed, axis=-1, keepdims=True))
    return (series_grad, jnp.sum(upstream * normed, axis=0))


def dot(a, b, dims=None):
    if dims is None:
        dims = (((1,), (0,)), ((), ()))
    return lax.dot_general(a, b, dims, preferred_element_type=f32)


def head_masks(scale):
    lane = lax.broadcasted_iota(jnp.int32, (1, LANES), 1)
    return [
        jnp.where((lane >= head * DH) & (lane < (head + 1) * DH), scale, 0.0).astype(bf16)
        for head in range(LANES // DH)
    ]


def causal_block():
    shape = (BLOCK, BLOCK)
    return lax.broadcasted_iota(jnp.int32, shape, 0) <= lax.broadcasted_iota(jnp.int32, shape, 1)


def attend_forward_kernel(query, keys, values, context, log_totals):
    masks = head_masks(DH**-0.5)
    seen = causal_block()
    values_t = values[...].astype(f32).T.astype(bf16)
    for i in range(SEQ_LEN // BLOCK):
        rows = slice(i * BLOCK, (i + 1) * BLOCK)
        parts = []
        for head, mask in enumerate(masks):
            piece = query[rows, :] * mask
            scores = [
                dot(keys[j * BLOCK : (j + 1) * BLOCK, :], piece, NT) for j in range(i + 1)
            ]
            scores[i] = jnp.where(seen, scores[i], masked_score)
            largest = jnp.max(scores[0], axis=0, keepdims=True)
            for block in scores[1:]:
                largest = jnp.maximum(largest, jnp.max(block, axis=0, keepdims=True))
            raised = [jnp.exp(block - largest) for block in scores]
            total = jnp.sum(raised[0], axis=0, keepdims=True)
            for block in raised[1:]:
                total = total + jnp.sum(block, axis=0, keepdims=True)
            summed = dot(
                values_t[head * DH : (head + 1) * DH, : (i + 1) * BLOCK],
                jnp.concatenate([block.astype(bf16) for block in raised], axis=0),
            )
            parts.append(summed / total)
            log_totals[0, head : head + 1, rows] = largest + jnp.log(total)
        context[rows, :] = jnp.concatenate(parts, axis=0).T.astype(bf16)


def attend_forward(project):
    pairs = project.shape[1] // (3 * LANES)
    column = lambda c: pl.BlockSpec((SEQ_LEN, LANES), lambda g, c=c: (0, c * pairs + g))
    heads = LANES // DH
    return pl.pallas_call(
        attend_forward_kernel,
        grid=(pairs,),
        in_specs=[column(0), column(1), column(2)],
        out_specs=[
            pl.BlockSpec((SEQ_LEN, LANES), lambda g: (0, g)),
            pl.BlockSpec((1, heads, SEQ_LEN), lambda g: (g, 0, 0)),
        ],
        out_shape=[
            jax.ShapeDtypeStruct((SEQ_LEN, pairs * LANES), bf16),
            jax.ShapeDtypeStruct((pairs, heads, SEQ_LEN), f32),
        ],
        compiler_params=pltpu.CompilerParams(vmem_limit_bytes=vmem_bytes),
        cost_estimate=estimate(14 << 30, 4 << 20),
        name="attend_forward",
    )(project, project, project)


def attend_backward_kernel(pairs, query, keys, values, upstream, log_totals, grads, key_sum, value_sum):
    g = pl.program_id(0)
    scaled_masks = head_masks(DH**-0.5)
    masks = head_masks(1.0)
    seen = causal_block()
    keys_t = keys[...].astype(f32).T.astype(bf16)
    key_sum[...] = jnp.zeros_like(key_sum)
    value_sum[...] = jnp.zeros_like(value_sum)
    for i in range(SEQ_LEN // BLOCK):
        rows = slice(i * BLOCK, (i + 1) * BLOCK)
        parts = []
        for head in range(LANES // DH):
            piece = query[rows, :] * scaled_masks[head]
            above = upstream[rows, :] * masks[head]
            log_total = log_totals[0, head : head + 1, rows]
            weights, probs = [], []
            inner = jnp.zeros((1, BLOCK), f32)
            for j in range(i + 1):
                columns = slice(j * BLOCK, (j + 1) * BLOCK)
                scores = dot(keys[columns, :], piece, NT)
                if j == i:
                    scores = jnp.where(seen, scores, masked_score)
                weights.append(jnp.exp(scores - log_total))
                probs.append(dot(values[columns, :], above, NT))
                inner = inner + jnp.sum(weights[j] * probs[j], axis=0, keepdims=True)
            score_grads = []
            for j in range(i + 1):
                score_grads.append((weights[j] * (probs[j] - inner)).astype(bf16))
            length = (i + 1) * BLOCK
            all_grads = jnp.concatenate(score_grads, axis=0)
            all_weights = jnp.concatenate([block.astype(bf16) for block in weights], axis=0)
            value_sum[:length, :] += dot(all_weights, above)
            key_sum[:length, :] += dot(all_grads, piece)
            parts.append(dot(keys_t[head * DH : (head + 1) * DH, :length], all_grads))
        query_grad = jnp.concatenate(parts, axis=0).T * DH**-0.5
        grads[rows, pl.ds(pl.multiple_of(g * LANES, LANES), LANES)] = query_grad.astype(bf16)
    grads[:, pl.ds(pl.multiple_of((pairs + g) * LANES, LANES), LANES)] = key_sum[...].astype(bf16)
    grads[:, pl.ds(pl.multiple_of((2 * pairs + g) * LANES, LANES), LANES)] = value_sum[...].astype(
        bf16
    )


def attend_backward(project, upstream, log_totals):
    pairs = project.shape[1] // (3 * LANES)
    column = lambda c: pl.BlockSpec((SEQ_LEN, LANES), lambda g, c=c: (0, c * pairs + g))
    heads = LANES // DH
    return pl.pallas_call(
        functools.partial(attend_backward_kernel, pairs),
        grid=(pairs,),
        in_specs=[
            column(0),
            column(1),
            column(2),
            column(0),
            pl.BlockSpec((1, heads, SEQ_LEN), lambda g: (g, 0, 0)),
        ],
        out_specs=pl.BlockSpec(project.shape, lambda g: (0, 0)),
        out_shape=jax.ShapeDtypeStruct(project.shape, bf16),
        scratch_shapes=[pltpu.VMEM((SEQ_LEN, LANES), f32), pltpu.VMEM((SEQ_LEN, LANES), f32)],
        compiler_params=pltpu.CompilerParams(vmem_limit_bytes=vmem_bytes),
        cost_estimate=estimate(20 << 30, 8 << 20),
        name="attend_backward",
    )(project, project, project, upstream, log_totals)


def slot_hits(place):
    return lax.broadcasted_iota(jnp.int32, (CAP, SEQ_LEN), 0) == place.astype(jnp.int32)


GROUP = 4


def keep_term(expert, onehots, terms, onehot, term):
    rows = pl.ds(pl.multiple_of(expert % GROUP * CAP, 64), CAP)
    onehots[rows, :] = onehot
    terms[rows, :] = term


def add_terms(expert, onehots, terms, total, results):
    @pl.when(expert % GROUP == GROUP - 1)
    def _():
        for i in range(SEQ_LEN // BLOCK):
            rows = slice(i * BLOCK, (i + 1) * BLOCK)
            term = dot(onehots[:, rows], terms[...], TN)

            @pl.when(expert == GROUP - 1)
            def _():
                total[rows, :] = term

            @pl.when(expert == EXPERTS - 1)
            def _():
                result = results[i // (SEQ_LEN // BLOCK // 2)]
                first = i % (SEQ_LEN // BLOCK // 2) * BLOCK
                result[first : first + BLOCK, :] = (total[rows, :] + term).astype(bf16)


def combine_scratch(width):
    return [
        pltpu.VMEM((GROUP * CAP, SEQ_LEN), bf16),
        pltpu.VMEM((GROUP * CAP, width), bf16),
        pltpu.VMEM((SEQ_LEN, width), f32),
    ]


def assemble(me, offsets, blocks, weight):
    rows = weight.shape[0] // len(offsets)
    for i, offset in enumerate(offsets):
        start = 0 if len(offsets) == 1 else pl.multiple_of((me ^ offset) * rows, 16)
        weight[pl.ds(start, rows), :] = blocks[i][0]


def fill(edge, parts, whole):
    rows = SEQ_LEN // 2
    for i, choices in enumerate(parts):
        target = slice(i * rows, (i + 1) * rows)
        if len(choices) == 1:
            whole[target, :] = choices[0][...]
            continue

        @pl.when(edge == 1)
        def _():
            whole[target, :] = choices[0][...]

        @pl.when(edge == 0)
        def _():
            whole[target, :] = choices[1][...]


def expert_kernel(offsets, choices, place_info, place, router, *refs):
    count = len(offsets[0])
    groups = []
    for _ in range(4):
        groups.append(refs[:choices])
        refs = refs[choices:]
    first_blocks, second_blocks = refs[:count], refs[count : 2 * count]
    back, back_two, gates, slots_in, slots_grad, activated, hidden_grad = refs[
        2 * count : 2 * count + 7
    ]
    onehots, terms, total, first, second, gate_grad, rows, upstream = refs[2 * count + 7 :]
    expert = pl.program_id(0)
    assemble(place_info[0], offsets[0], first_blocks, first)
    assemble(place_info[0], offsets[1], second_blocks, second)

    @pl.when(expert == 0)
    def _():
        fill(place_info[1], groups[:2], rows)
        fill(place_info[1], groups[2:], upstream)
        logits = dot(router[...], rows[...], NT)
        chosen = place[...] >= 0.0
        largest = jnp.max(jnp.where(chosen, logits, masked_score), axis=0, keepdims=True)
        raised = jnp.where(chosen, jnp.exp(jnp.where(chosen, logits - largest, 0.0)), 0.0)
        gates[...] = raised / jnp.sum(raised, axis=0, keepdims=True)

    row = pl.ds(expert, 1)
    hits = slot_hits(place[row, :])
    onehot = jnp.where(hits, 1.0, 0.0).astype(bf16)
    entered = dot(onehot, rows[...]).astype(bf16)
    above = dot(onehot, upstream[...]).astype(bf16)
    slot_gate = jnp.sum(jnp.where(hits, gates[row, :], 0.0), axis=1, keepdims=True)
    slots_in[0] = entered
    slots_grad[0] = above
    factor = 0.7978845608028654
    width = first.shape[1]
    chunk = BLOCK if width % BLOCK == 0 else width
    products = []
    for start in range(0, width, chunk):
        part = slice(start, start + chunk)
        products.append((part, dot(entered, first[:, part]), dot(above, second[:, part])))
    slot_gate_grad = jnp.zeros((CAP, 1), f32)
    parts = []
    for part, hidden, raw_grad in products:
        square = hidden * hidden
        half = 0.5 + 0.5 * jnp.tanh(hidden * (factor + factor * 0.044715 * square))
        active = hidden * half
        slope = half + active * (1.0 - half) * (2 * factor + 6 * factor * 0.044715 * square)
        active = active.astype(bf16).astype(f32)
        activated[0, :, part] = (slot_gate * active).astype(bf16)
        slot_gate_grad = slot_gate_grad + jnp.sum(active * raw_grad, axis=1, keepdims=True)
        below = (slot_gate * raw_grad * slope).astype(bf16)
        hidden_grad[0, :, part] = below
        parts.append(below)
    gate_grad[row, :] = jnp.sum(jnp.where(hits, slot_gate_grad, 0.0), axis=0, keepdims=True)
    below = jnp.concatenate(parts, axis=1)
    slot_back = dot(below, first[...], NT).astype(bf16)
    keep_term(expert, onehots, terms, onehot, slot_back)
    add_terms(expert, onehots, terms, total, (back, back_two))

    @pl.when(expert == EXPERTS - 1)
    def _():
        half = SEQ_LEN // 2
        for i, result in enumerate((back, back_two)):
            result[half:, :] = jnp.zeros((result.shape[0] - half, result.shape[1]), bf16)
            grads = gate_grad[:, i * half : (i + 1) * half]
            result[half:, :half] = jnp.concatenate([grads, jnp.zeros_like(grads)], 0).astype(bf16)


def block_specs(blocks):
    return [pl.BlockSpec((1,) + block.shape[1:], lambda e: (e, 0, 0)) for block in blocks]


def estimate(flops, moved):
    return pl.CostEstimate(flops=flops, bytes_accessed=moved, transcendentals=0)


scalar = pl.BlockSpec(memory_space=pltpu.SMEM)


def through_experts(place_info, place, router, row_parts, upstream_parts, first, second):
    parts = row_parts + upstream_parts
    choices = len(parts[0])
    half, width = parts[0][0].shape
    hidden_width = first[1][0].shape[2]
    line = pl.BlockSpec((EXPERTS, SEQ_LEN), lambda e: (0, 0))
    whole = pl.BlockSpec((half, width), lambda e: (0, 0))
    under = pl.BlockSpec((half + 16, width), lambda e: (0, 0))
    slots = lambda columns: pl.BlockSpec((1, CAP, columns), lambda e: (e, 0, 0))
    slot_shape = lambda columns: jax.ShapeDtypeStruct((EXPERTS, CAP, columns), bf16)
    return pl.pallas_call(
        functools.partial(expert_kernel, (first[0], second[0]), choices),
        grid=(EXPERTS,),
        in_specs=[scalar, line, pl.BlockSpec((EXPERTS, width), lambda e: (0, 0))]
        + [whole] * (4 * choices)
        + block_specs(first[1])
        + block_specs(second[1]),
        out_specs=[
            under,
            under,
            line,
            slots(width),
            slots(width),
            slots(hidden_width),
            slots(hidden_width),
        ],
        out_shape=[
            jax.ShapeDtypeStruct((half + 16, width), bf16),
            jax.ShapeDtypeStruct((half + 16, width), bf16),
            jax.ShapeDtypeStruct((EXPERTS, SEQ_LEN), f32),
            slot_shape(width),
            slot_shape(width),
            slot_shape(hidden_width),
            slot_shape(hidden_width),
        ],
        scratch_shapes=combine_scratch(width)
        + [
            pltpu.VMEM((width, hidden_width), bf16),
            pltpu.VMEM((width, hidden_width), bf16),
            pltpu.VMEM((EXPERTS, SEQ_LEN), f32),
            pltpu.VMEM((SEQ_LEN, width), bf16),
            pltpu.VMEM((SEQ_LEN, width), bf16),
        ],
        compiler_params=pltpu.CompilerParams(vmem_limit_bytes=vmem_bytes),
        cost_estimate=estimate(60 << 30, 50 << 20),
        name="through_experts",
    )(place_info, place, router, *[item for part in parts for item in part], *first[1], *second[1])


def grads_kernel(count, parts, place_info, *refs):
    slots_in, slots_grad, activated, hidden_grad = [
        jnp.concatenate([ref[0] for ref in refs[i * count : (i + 1) * count]], axis=0)
        for i in range(4)
    ]
    outs = refs[4 * count :]
    even = (place_info[0] & 1) == 0
    for i, (left, right) in enumerate(((slots_in, hidden_grad), (slots_grad, activated))):
        product = dot(left, right, TN)
        if parts == 1:
            outs[i][0, 0] = product.astype(bf16)
            continue
        rows = product.shape[0] // parts
        for j in range(parts // 2):
            one = product[2 * j * rows : (2 * j + 1) * rows]
            two = product[(2 * j + 1) * rows : (2 * j + 2) * rows]
            outs[2 * i][0, j] = jnp.where(even, one, two).astype(bf16)
            outs[2 * i + 1][0, j] = jnp.where(even, two, one).astype(bf16)


def expert_grads(place_info, sequences, parts):
    count = len(sequences)
    width, hidden_width = sequences[0][0].shape[2], sequences[0][2].shape[2]
    slots = lambda columns: pl.BlockSpec((1, CAP, columns), lambda e: (e, 0, 0))
    specs = [slots(width), slots(width), slots(hidden_width), slots(hidden_width)]
    shape = (max(parts // 2, 1), width // parts, hidden_width)
    outs = 2 * min(parts, 2)
    return pl.pallas_call(
        functools.partial(grads_kernel, count, parts),
        grid=(EXPERTS,),
        in_specs=[scalar] + [spec for spec in specs for _ in range(count)],
        out_specs=[pl.BlockSpec((1,) + shape, lambda e: (e, 0, 0, 0))] * outs,
        out_shape=[jax.ShapeDtypeStruct((EXPERTS,) + shape, bf16)] * outs,
        compiler_params=pltpu.CompilerParams(vmem_limit_bytes=vmem_bytes),
        cost_estimate=estimate(50 << 30, 50 << 20),
        name="expert_grads",
    )(place_info, *[item[i] for i in range(4) for item in sequences])


def outputs_kernel(count, offsets, place_info, *refs):
    expert = pl.program_id(0)
    blocks_count = len(offsets)
    place, activated = refs[:count], refs[count : 2 * count]
    blocks = refs[2 * count : 2 * count + blocks_count]
    refs = refs[2 * count + blocks_count :]
    second = refs[-1]
    assemble(place_info[0], offsets, blocks, second)
    for s in range(count):
        hits = slot_hits(place[s][pl.ds(expert, 1), :])
        out = dot(activated[s][0], second[...], NT).astype(bf16)
        onehot = jnp.where(hits, 1.0, 0.0).astype(bf16)
        onehots, terms, total = refs[2 * count + 3 * s : 2 * count + 3 * s + 3]
        keep_term(expert, onehots, terms, onehot, out)
        add_terms(expert, onehots, terms, total, refs[2 * s : 2 * s + 2])


def expert_outputs(place_info, places, activated, second):
    count = len(places)
    hidden_width = second[1][0].shape[2]
    width = second[1][0].shape[1] * len(second[0])
    half = SEQ_LEN // 2
    line = pl.BlockSpec((EXPERTS, SEQ_LEN), lambda e: (0, 0))
    whole = pl.BlockSpec((half, width), lambda e: (0, 0))
    slots = pl.BlockSpec((1, CAP, hidden_width), lambda e: (e, 0, 0))
    return pl.pallas_call(
        functools.partial(outputs_kernel, count, second[0]),
        grid=(EXPERTS,),
        in_specs=[scalar] + [line] * count + [slots] * count + block_specs(second[1]),
        out_specs=[whole] * (2 * count),
        out_shape=[jax.ShapeDtypeStruct((half, width), bf16)] * (2 * count),
        scratch_shapes=combine_scratch(width) * count + [pltpu.VMEM((width, hidden_width), bf16)],
        compiler_params=pltpu.CompilerParams(vmem_limit_bytes=vmem_bytes),
        cost_estimate=estimate(60 << 30, 30 << 20),
        name="expert_outputs",
    )(place_info, *places, *activated, *second[1])


def from_partner(value, distance):
    return lax.ppermute(value, "tensor", [(i, i ^ distance) for i in range(4)])


def between(value, *pairs):
    return lax.ppermute(value, "tensor", list(pairs))


def from_group(value, distance):
    count = lax.axis_size("dp")
    return lax.ppermute(value, "dp", [(i, i ^ distance) for i in range(count)])


def after(value, *others):
    return lax.optimization_barrier((value,) + others)[0]


def all_after(values, *others):
    return lax.optimization_barrier(tuple(values) + others)[: len(values)]


def summed(items):
    total = items[0].astype(f32)
    for item in items[1:]:
        total = total + item.astype(f32)
    return total


def spread_near(mine):
    return (mine, from_partner(mine, 1), between(mine, (1, 2), (2, 1)))


def spread_far(near):
    mine, partner, middle = near
    far = between(after(mine, partner, middle), (0, 3), (3, 0))
    return (
        between(middle, (1, 0), (2, 3)),
        between(partner, (1, 2), (2, 1)),
        far,
        middle,
    )


def collect_start(two, three):
    far = between(three, (0, 3), (3, 0))
    inward = between(two, (0, 1), (3, 2))
    across = between(two, (1, 2), (2, 1))
    return far, inward, across


def collect_middle(three, started):
    return between(summed([three, started[1]]).astype(bf16), (1, 2), (2, 1))


def collect_end(mine, partner, started, middle, edge, waits=()):
    far, _, across = started
    partner = jnp.where(edge, partner, summed([partner, across]).astype(bf16))
    received, middle = all_after([from_partner(partner, 1), middle], *waits)
    return summed([mine, received, jnp.where(edge, far, middle)])


def grouped(block):
    return lax.axis_size("dp") == 8 and block.shape[1] % 16 == 0


def gathered(blocks):
    if len(blocks) > 1:
        blocks.update({offset ^ 1: from_group(item, 1) for offset, item in list(blocks.items())})
    return (tuple(blocks), list(blocks.values()))


def scatter_step(me, items, axis, distance):
    bit = (me // distance) & 1
    take = lambda item, which: lax.dynamic_index_in_dim(item, which, axis, keepdims=False)
    sent = summed([take(item, 1 - bit) for item in items]).astype(bf16)
    return [take(item, bit) for item in items], sent


def scatter_start(me, kept, received, way):
    items = [item.reshape((EXPERTS, 2, 2) + item.shape[2:]) for item in (kept, received)]
    return scatter_step(me, items, 1 if way[0] == 4 else 2, way[0])


def shards(
    tokens,
    cotangent,
    routes,
    gain_attention,
    gain_experts,
    router_weight,
    qkv_weight,
    proj_weight,
    expert_in,
    expert_back,
):
    local_rows, width = tokens.shape
    group_rows = routes.shape[0]
    sequences = group_rows // SEQ_LEN
    depth, _, quarter = qkv_weight.shape
    part = depth // 4
    side = 2 * quarter
    place_z = lax.axis_index("tensor")
    me = lax.axis_index("dp")
    odd = (place_z & 1) == 1
    low = place_z < 2
    half = place_z & 1
    edge = (place_z == 0) | (place_z == 3)

    def ordered(mine, other):
        return jnp.where(
            odd,
            jnp.concatenate([other, mine], axis=0),
            jnp.concatenate([mine, other], axis=0),
        )

    small = jnp.concatenate([gain_attention[:, None], gain_experts[:, None], router_weight], axis=1)
    small = jnp.pad(small, ((0, depth - part), (0, LANES - small.shape[1])))
    mine = qkv_weight.reshape(depth, 3 * quarter)
    small = small[:part]
    across = from_partner(mine, 2)
    smalls = [small] + [from_partner(small, distance) for distance in (1, 2, 3)]
    pick = lambda items: (
        jnp.where(low, items[0], items[2]),
        jnp.where(low, items[2], items[0]),
        jnp.where(low, items[1], items[3]),
        jnp.where(low, items[3], items[1]),
    )
    smalls = pick(smalls)
    smalls = jnp.where(
        odd,
        jnp.concatenate([smalls[2], smalls[0], smalls[3], smalls[1]], axis=0),
        jnp.concatenate([smalls[0], smalls[2], smalls[1], smalls[3]], axis=0),
    )
    one = jnp.where(low, mine, across).reshape(depth, 3, quarter)
    two = jnp.where(low, across, mine).reshape(depth, 3, quarter)
    packed = jnp.concatenate(
        [jnp.concatenate([one, two], axis=2).reshape(depth, 3 * side), smalls], axis=1
    )
    ways = ((2, 4), (4, 2))
    blocks = [expert_in, expert_back.transpose(0, 2, 1)]
    split = grouped(blocks[0])
    if split:
        crossed = [from_group(block, way[0]) for block, way in zip(blocks, ways)]
    packed = lax.all_gather(packed, "dp", axis=0, tiled=True)
    qkv_matrix = packed[:, : 3 * side]
    small = packed[:, 3 * side :]
    attn_gain = small[:, 0].astype(f32)
    moe_gain = small[:, 1].astype(f32)
    router = small[:, 2 : 2 + EXPERTS]
    token_partner = from_partner(after(tokens, across), 1)
    projection = after(proj_weight.T, token_partner)
    projections = [projection] + [from_partner(projection, distance) for distance in (1, 2, 3)]
    proj_matrix = jnp.concatenate(pick(projections), axis=1)
    proj_matrix = lax.all_gather(proj_matrix, "dp", axis=0, tiled=True)

    names = jnp.arange(EXPERTS, dtype=jnp.int32)[:, None]
    chosen = (routes[:, 0][None, :] == names) | (routes[:, 1][None, :] == names)
    by_sequence = chosen.reshape(EXPERTS * sequences, SEQ_LEN)
    order = jnp.arange(SEQ_LEN, dtype=jnp.int32)
    earlier = (order[:, None] < order[None, :]).astype(bf16)
    counts = dot(by_sequence.astype(bf16), earlier)
    places = jnp.where(by_sequence, counts, -1.0).reshape(EXPERTS, sequences, 2, local_rows)
    places = jnp.where(odd, places[:, :, ::-1], places)
    places = jnp.where(low, places, places[:, ::-1]).reshape(EXPERTS, sequences, SEQ_LEN)
    places = [places[:, s] for s in range(sequences)]

    sequence = ordered(tokens, token_partner)
    sequence, *places = lax.optimization_barrier((sequence, *places))
    if split:
        sequence, *crossed = lax.optimization_barrier((sequence, *crossed))
        seconds = [
            from_group(after(block, other), way[1])
            for block, other, way in zip(blocks, crossed, ways)
        ]
    out_near = spread_near(after(cotangent, token_partner))
    normed = norm_rows(sequence.astype(f32), attn_gain).astype(bf16)
    project = dot(normed, qkv_matrix).astype(bf16)
    router_t = router.T
    project, router_t, *near = lax.optimization_barrier((project, router_t) + out_near[1:])
    out_near = out_near[:1] + tuple(near)
    out_far = spread_far(out_near)
    context, log_totals = attend_forward(project)
    if split:
        context, *seconds = lax.optimization_barrier((context, *seconds))
        thirds = [
            from_group(after(other, second), way[1])
            for other, second, way in zip(crossed, seconds, ways)
        ]
    kept = lax.dynamic_slice_in_dim(context, half * local_rows, local_rows, 0)
    sent = lax.dynamic_slice_in_dim(context, (1 - half) * local_rows, local_rows, 0)
    context = jnp.concatenate([kept, from_partner(sent, 1)], axis=1)
    inputs = tokens.astype(f32)
    middle = inputs + dot(context, proj_matrix, NT)
    moe_normed = norm_rows(middle, moe_gain).astype(bf16)
    moe_near = lax.optimization_barrier(
        spread_near(moe_normed) + (tuple(thirds) if split else ())
    )
    moe_near, thirds = moe_near[:3], moe_near[3:]
    if split:
        weights = [
            {0: block, one: first, two: second, one ^ two: third}
            for block, first, second, third, (one, two) in zip(
                blocks, crossed, seconds, thirds, ways
            )
        ]
    else:
        weights = [{0: lax.all_gather(block, "dp", axis=1, tiled=True)} for block in blocks]
    expert_first, expert_second = (gathered(item) for item in weights)
    moe_far = spread_far(moe_near)

    place_info = jnp.stack([me, edge.astype(jnp.int32)]).astype(jnp.int32)
    run = lambda s, rows, upstream: through_experts(
        place_info, places[s], router_t, rows, upstream, expert_first, expert_second
    )
    halves = lambda near: [(item,) for item in near[:2]]
    own = run(0, halves(moe_near), halves(out_near))
    own_outs = expert_outputs(place_info, places[:1], [own[5]], expert_second)
    late = all_after(moe_far + out_far, own_outs[0])
    choices = lambda far: [far[:2], far[2:]]
    other = run(1, choices(late[:4]), choices(late[4:]))
    started = collect_start(other[0], other[1])
    line = lambda item, i: item[:, i * local_rows : (i + 1) * local_rows]
    parts = 8 if split else 1
    grads = expert_grads(place_info, [item[3:] for item in (own, other)], parts)
    activated = all_after([other[5]], grads[0])
    other_outs = expert_outputs(place_info, places[1:], activated, expert_second)
    started = all_after(started, other_outs[0])
    middle_back = collect_middle(other[1], started)
    outs = list(own_outs) + list(other_outs)
    waits = ()
    if split:
        received = [from_group(grads[i], 1) for i in (1, 3)]
        received = all_after(received, other_outs[0])
        scattering = [
            scatter_start(me, grads[2 * i], received[i], way) for i, way in enumerate(ways)
        ]
        waits = lax.optimization_barrier(tuple(item[1] for item in scattering))
        scattering = [(item[0], value) for item, value in zip(scattering, waits)]
    collected = collect_end(own[0], own[1], started, middle_back, edge, waits)
    moe_back, gate_grad = collected[:local_rows], collected[local_rows : local_rows + EXPERTS, :local_rows]

    out_grad = cotangent.astype(f32)
    local_gates = line(own[2], 0)
    logit_grad = local_gates * (
        gate_grad - jnp.sum(local_gates * gate_grad, axis=0, keepdims=True)
    )
    logit_grad = logit_grad.astype(bf16)
    router_grad = dot(moe_normed, logit_grad, (((0,), (1,)), ((), ())))
    router_back = dot(logit_grad, router, (((0,), (1,)), ((), ())))
    middle_norm, moe_gain_grad = norm_back(middle, moe_gain, moe_back + router_back)
    middle_grad = out_grad + middle_norm
    attn_grad = middle_grad.astype(bf16)
    context_grad = dot(attn_grad, proj_matrix).astype(bf16)
    context_partner = from_partner(context_grad[:, side:], 1)
    context_grad = ordered(context_grad[:, :side], context_partner)
    if split:
        received = [from_group(item[1], way[0]) for item, way in zip(scattering, ways)]
    proj_grad = dot(attn_grad, context, TN)
    project_grad = attend_backward(project, context_grad, log_totals)
    sent = lax.dynamic_slice_in_dim(project_grad, (1 - half) * local_rows, local_rows, 0)
    kept = lax.dynamic_slice_in_dim(project_grad, half * local_rows, local_rows, 0)
    qkv_grad = dot(normed, project_grad, TN)
    outs = all_after(outs, context_partner)
    started = collect_start(outs[2], outs[3])
    if split:
        qkv_grad, *started = lax.optimization_barrier((qkv_grad, *started, *received))
        started, received = started[:3], started[3:]
    arrived = from_partner(dot(sent, qkv_matrix, NT).astype(bf16), 1)
    if split:
        scattering = [
            scatter_step(me, item[0] + [value], 1, way[1])
            for item, value, way in zip(scattering, received, ways)
        ]
        arrived, *sent = lax.optimization_barrier(
            (arrived,) + tuple(item[1] for item in scattering)
        )
    attn_back = dot(kept, qkv_matrix, NT) + arrived.astype(f32)
    if split:
        received = [from_group(item, way[1]) for item, way in zip(sent, ways)]
        kept_sums = all_after([summed(item[0]) for item in scattering], attn_back)
        first_total, second_total = (
            kept + value.astype(f32) for kept, value in zip(kept_sums, received)
        )
    else:
        first_total, second_total = (
            lax.psum_scatter(item[0][:, 0], "dp", scatter_dimension=1, tiled=True).astype(f32)
            for item in (grads[:1], grads[1:])
        )
    second_total = second_total.transpose(0, 2, 1)
    input_norm, _ = norm_back(inputs, attn_gain, attn_back)
    input_grad = middle_grad + input_norm

    scaled_gain_grad = jnp.sum(qkv_grad * qkv_matrix.astype(f32), axis=1, keepdims=True)
    small_grad = jnp.concatenate([scaled_gain_grad, moe_gain_grad[:, None], router_grad], 1)
    small_grad = jnp.pad(small_grad, ((0, 0), (0, LANES - small_grad.shape[1])))
    summed_late = lax.psum_scatter(
        jnp.concatenate([qkv_grad, proj_grad, small_grad], axis=1).astype(bf16),
        "dp",
        scatter_dimension=0,
        tiled=True,
    )

    waits = tuple(received) if split else ()
    ended = collect_end(outs[0], outs[1], started, collect_middle(outs[3], started), edge, waits)
    result = middle + ended

    qkv_part = summed_late[:, : 3 * side].reshape(depth, 3, 2, quarter)
    proj_part = summed_late[:, 3 * side : 3 * side + 4 * quarter].reshape(depth, 4, quarter)
    small_part = summed_late[:, 3 * side + 4 * quarter :].reshape(4, part, LANES)

    def message(distance):
        pieces = {0: (0, 1), 1: (2, 3), 2: (1, 0), 3: (3, 2)}[distance]
        proj_piece = jnp.where(low, proj_part[:, pieces[0]], proj_part[:, pieces[1]])
        small_piece = lax.dynamic_slice_in_dim(small_part, place_z ^ distance, 1, 0)[0]
        small_piece = jnp.pad(small_piece, ((0, depth - part), (0, 0)))
        items = [proj_piece, small_piece]
        if distance in (0, 2):
            qkv_piece = jnp.where(low, qkv_part[:, :, pieces[0]], qkv_part[:, :, pieces[1]])
            items.append(qkv_piece.reshape(depth, 3 * quarter))
        return jnp.concatenate(items, axis=1)

    total = summed([message(0), from_partner(message(2), 2)])
    split_at = quarter + LANES
    shared = summed(
        [total[:, :split_at]] + [from_partner(message(distance), distance) for distance in (1, 3)]
    )
    qkv_total = total[:, split_at:].reshape(depth, 3, quarter)
    proj_total = shared[:, :quarter].T
    small_total = shared[:part, quarter:]
    gain_total = small_total[:, 0] / gain_attention.astype(f32)
    return (
        result,
        input_grad,
        gain_total,
        small_total[:, 1],
        small_total[:, 2 : 2 + EXPERTS],
        qkv_total,
        proj_total,
        first_total,
        second_total,
    )


def solution(mesh):
    in_specs = (
        P(("dp", "tensor"), None),
        P(("dp", "tensor"), None),
        P("dp", None),
        P(("dp", "tensor")),
        P(("dp", "tensor")),
        P(("dp", "tensor"), None),
        P("dp", None, "tensor"),
        P("tensor", "dp"),
        P(None, "dp", "tensor"),
        P(None, "tensor", "dp"),
    )
    out_specs = (
        P(("dp", "tensor"), None),
        P(("dp", "tensor"), None),
        P(("dp", "tensor")),
        P(("dp", "tensor")),
        P(("dp", "tensor"), None),
        P("dp", None, "tensor"),
        P("tensor", "dp"),
        P(None, "dp", "tensor"),
        P(None, "tensor", "dp"),
    )
    return jax.shard_map(shards, mesh=mesh, in_specs=in_specs, out_specs=out_specs, check_vma=False)
```
